32 devices in a mesh: ctx: 8 (over z, core), head: 4 (over y, x).
Axes of the slice: x: 2, y: 2, z: 4, core: 2. Of those that a mesh axis runs over, the one named last changes fastest.
Arguments:
- q_nope: bfloat16 [1024, 8192], P('ctx', 'head'), may hold values from -6 to 6
- q_rope: bfloat16 [1024, 4096], P('ctx', 'head'), may hold values from -80 to 80
- kv_cache: bfloat16 [1024, 576], P('ctx'), may hold values from -180 to 180
- kv_gain: bfloat16 [512], replicated, may hold values from 0.099609375 to 1.8984375
- w_uk: bfloat16 [64, 128, 512], P('head'), may hold values from -0.5 to 0.5
- w_uv: bfloat16 [64, 512, 128], P('head'), may hold values from -0.25 to 0.25
- attn_out: bfloat16 [1024, 8192], P('ctx', 'head'), may hold values from -6 to 6
- d_out: bfloat16 [1024, 8192], P('ctx', 'head'), may hold values from -6 to 6
- span_table: int32 [8, 2], replicated, may hold values from 0 to 15, as said below
Outputs:
- d_q_nope: bfloat16 [1024, 8192], P('ctx', 'head')
- d_q_rope: bfloat16 [1024, 4096], P('ctx', 'head')
- d_cache: float32 [1024, 576], P('ctx')
The draws below stay inside these ranges and needn't reach their ends.
Inputs may be any that keep to these rules, and one draw needn't show every extreme that they name: `span_table`: row d lists the two blocks of 64 positions held by the rows of ctx index d, in this order: a block c below 8, then its mirror 16 - 1 - c. The first column is a permutation.
All inputs are finite; a program needn't handle non-finite values.
Results may differ from the reference program's by a relative error of at most 0.02.
Values may be sent and summed in bfloat16 or wider, within the bound.
No kernel may reach another device: no remote copies, remote signals or barrier semaphores. Data moves between devices by JAX's collectives and lax.ppermute only.
A program may use at most 64 MiB of HBM per device.

```python
import jax
import jax.numpy as jnp
from jax import lax

D_LAT = 512
D_ROPE = 64
D_NOPE = 128
D_V = 128
HEADS = 64
TOK_DEV = 128
SPAN = 64
TOKENS = 1024
N_CTX = 8
N_HEAD = 4


def rope_source(key):
    normal_part = jax.random.normal(jax.random.fold_in(key, 101), (TOKENS, D_ROPE), jnp.float32)
    return normal_part


def draw_kv_cache(key, part):
    normal_rope = rope_source(key)
    key = jax.random.fold_in(key, 1)
    rope_part = jnp.clip(normal_rope, -4.0, 4.0)
    latent = jnp.clip(jax.random.normal(jax.random.fold_in(key, 4), (TOKENS, D_LAT), jnp.float32), -4.0, 4.0)
    return jnp.concatenate([latent, rope_part], axis=1).astype(jnp.bfloat16)


def draw_q_rope(key, part):
    key = jax.random.fold_in(key, 5)
    values = jnp.clip(jax.random.normal(jax.random.fold_in(key, 6), (TOKENS, HEADS, D_ROPE), jnp.float32), -4.0, 4.0)
    return values.reshape(TOKENS, HEADS * D_ROPE).astype(jnp.bfloat16)


def draw_span_table(key, part):
    key = jax.random.fold_in(key, 9)
    block_count = TOKENS // TOK_DEV
    order = jax.random.permutation(key, block_count).astype(jnp.int32)
    return jnp.stack([order, 2 * block_count - 1 - order], axis=1).astype(jnp.int32)


def levels(key, shape, shards, low, largest):
    gain, own = 1.0, jax.random.fold_in(key, 6)
    for position, shards_of in shards:
        heights = jnp.exp(jax.random.uniform(jax.random.fold_in(own, position), (shards_of,), jnp.float32, low / len(shards), largest / len(shards)))
        gain = gain * jnp.repeat(heights, shape[position] // shards_of).reshape([-1 if axis == position else 1 for axis in range(len(shape))])
    return gain


def centred(stream_key, shape, scale, bound, shards=(), kind=jnp.bfloat16):
    gain = levels(stream_key, shape, shards, -0.22, 0.18) if shards else 1.0
    result = jax.random.normal(stream_key, shape, jnp.float32) * scale * gain
    return jnp.minimum(jnp.maximum(result, -bound), bound).astype(kind)


def setup_inputs(seed: int = 0) -> dict:
    seeds = jax.random.split(jax.random.key(seed), 10)
    q_nope = centred(seeds[0], (TOKENS, HEADS * D_NOPE), 1.0, 6.0, ((0, 8), (1, 4)))
    q_rope = draw_q_rope(jax.random.fold_in(seeds[9], 71), 0)
    kv_cache = draw_kv_cache(jax.random.fold_in(seeds[9], 71), 0)
    kv_gain = jnp.clip(1.0 + 0.18 * jax.random.normal(seeds[3], (D_LAT,), jnp.float32), 0.099609375, 1.8984375).astype(jnp.bfloat16)
    w_uk = centred(seeds[4], (HEADS, D_NOPE, D_LAT), D_NOPE ** -0.5, 0.5, ((0, 4),))
    w_uv = centred(seeds[5], (HEADS, D_LAT, D_V), D_LAT ** -0.5, 0.25, ((0, 4),))
    attn_out = centred(seeds[6], (TOKENS, HEADS * D_V), 1.0, 6.0, ((0, 8), (1, 4)))
    d_out = centred(seeds[7], (TOKENS, HEADS * D_V), 1.0, 6.0, ((0, 8), (1, 4)))
    span_table = draw_span_table(jax.random.fold_in(seeds[9], 71), 0)
    return dict(q_nope=q_nope, q_rope=q_rope, kv_cache=kv_cache, kv_gain=kv_gain, w_uk=w_uk, w_uv=w_uv, attn_out=attn_out, d_out=d_out, span_table=span_table)


eps_norm = 1e-06

def rounded(values):
    return lax.optimization_barrier(values.astype(jnp.bfloat16)).astype(jnp.float32)

def reference(q_nope, q_rope, kv_cache, kv_gain, w_uk, w_uv, attn_out, d_out, span_table):
    score_scale = float(D_NOPE + D_ROPE) ** (-0.5)
    head_group = HEADS // N_HEAD
    gain_rows = kv_gain.astype(jnp.float32)
    raw_rows = kv_cache[:, :D_LAT].astype(jnp.float32)
    inverse = lax.rsqrt(lax.optimization_barrier(jnp.mean(raw_rows * raw_rows, axis=1, keepdims=True)) + eps_norm)
    latent = (raw_rows * inverse * gain_rows).astype(jnp.bfloat16)
    key_cat = jnp.concatenate([latent, kv_cache[:, D_LAT:]], axis=1).astype(jnp.float32)
    key_lat = key_cat[:, :D_LAT]
    row_ids = jnp.arange(TOKENS, dtype=jnp.int32)
    positions = (span_table.reshape(-1)[row_ids // SPAN] * SPAN + row_ids % SPAN).astype(jnp.int32)
    w_uk_wide = w_uk.astype(jnp.float32)
    nope_rows = q_nope.reshape(TOKENS, HEADS, D_NOPE).astype(jnp.float32)
    q_latent = jnp.einsum('thn,hnl->thl', nope_rows, w_uk_wide).astype(jnp.bfloat16)
    queries = jnp.concatenate([q_latent, q_rope.reshape(TOKENS, HEADS, D_ROPE)], axis=2)
    grad_rows = d_out.reshape(TOKENS, HEADS, D_V).astype(jnp.float32)
    d_latent = jnp.einsum('thv,hlv->thl', grad_rows, w_uv.astype(jnp.float32)).astype(jnp.bfloat16)
    row_delta = lax.optimization_barrier(jnp.sum(grad_rows * attn_out.reshape(TOKENS, HEADS, D_V).astype(jnp.float32), axis=2))

    def source(key_total, source_index):
        row_start = source_index * TOK_DEV
        query_rows = lax.dynamic_slice_in_dim(queries, row_start, TOK_DEV, 0).astype(jnp.float32)
        latent_grads = lax.dynamic_slice_in_dim(d_latent, row_start, TOK_DEV, 0).astype(jnp.float32)
        delta_rows = lax.dynamic_slice_in_dim(row_delta, row_start, TOK_DEV, 0)
        query_pos = lax.dynamic_slice_in_dim(positions, row_start, TOK_DEV, 0)
        scores = jnp.einsum('thd,kd->htk', query_rows, key_cat) * score_scale
        visible = positions[None, None, :] <= query_pos[None, :, None]
        scores = jnp.where(visible, scores, -jnp.inf)
        row_top = lax.optimization_barrier(jnp.max(scores, axis=2, keepdims=True))
        log_total = row_top + jnp.log(lax.optimization_barrier(jnp.sum(jnp.exp(scores - row_top), axis=2, keepdims=True)))
        attn_prob = jnp.exp(scores - log_total)
        prob_round = rounded(attn_prob)
        d_prob = jnp.einsum('thl,kl->htk', latent_grads, key_lat)
        d_score = rounded(attn_prob * (d_prob - jnp.transpose(delta_rows)[:, :, None]) * score_scale)
        d_query = jnp.einsum('htk,kd->thd', d_score, key_cat)
        group_score = d_score.reshape(N_HEAD, head_group, TOK_DEV, TOKENS)
        group_prob = prob_round.reshape(N_HEAD, head_group, TOK_DEV, TOKENS)
        group_query = query_rows.reshape(TOK_DEV, N_HEAD, head_group, D_LAT + D_ROPE)
        group_grad = latent_grads.reshape(TOK_DEV, N_HEAD, head_group, D_LAT)
        key_part = jnp.einsum('ghtk,tghd->gkd', group_score, group_query)
        prob_part = jnp.einsum('ghtk,tghl->gkl', group_prob, group_grad)
        key_part = jnp.concatenate([key_part[:, :, :D_LAT] + prob_part, key_part[:, :, D_LAT:]], axis=2)
        key_total = key_total + lax.optimization_barrier(jnp.sum(rounded(key_part), axis=0))
        d_nope = jnp.einsum('thl,hnl->thn', rounded(d_query[:, :, :D_LAT]), w_uk_wide).astype(jnp.bfloat16)
        d_rope = d_query[:, :, D_LAT:].astype(jnp.bfloat16)
        return (key_total, (d_nope, d_rope))
    start_total = jnp.zeros((TOKENS, D_LAT + D_ROPE), jnp.float32)
    key_total, (d_nope, d_rope) = lax.scan(source, start_total, jnp.arange(N_CTX, dtype=jnp.int32))
    scaled = key_total[:, :D_LAT] * gain_rows
    inner_mean = lax.optimization_barrier(jnp.mean(raw_rows * scaled, axis=1, keepdims=True))
    d_raw = inverse * scaled - raw_rows * inverse * inverse * inverse * inner_mean
    d_cache = jnp.concatenate([d_raw, key_total[:, D_LAT:]], axis=1)
    return (d_nope.reshape(TOKENS, HEADS * D_NOPE), d_rope.reshape(TOKENS, HEADS * D_ROPE), d_cache)
```

```python
import functools

import jax
import jax.numpy as jnp
from jax import lax
from jax.experimental import pallas as pl
from jax.experimental.pallas import tpu as pltpu
from jax.sharding import PartitionSpec as P

neg_big = -1e30
eps_norm = 1e-06
log2_e = 1.4426950408889634
key_tile = 256
mib = 1024 * 1024
wide_mib = 53
fetch_mib = 54
query_mib = 51
delta_rows = 16
fetch_ahead = 3
row_chunk = 256
f32 = jnp.float32
bf16 = jnp.bfloat16
in_vmem = pl.BlockSpec(memory_space=pltpu.VMEM)
in_hbm = pl.BlockSpec(memory_space=pltpu.HBM)
in_any = pl.BlockSpec(memory_space=pl.ANY)
in_smem = pl.BlockSpec(memory_space=pltpu.SMEM)


def dot_nn(left, right):
    return lax.dot_general(left, right, (((1,), (0,)), ((), ())), preferred_element_type=f32)


def dot_nt(left, right):
    return lax.dot_general(left, right, (((1,), (1,)), ((), ())), preferred_element_type=f32)


def dot_tn(left, right):
    return lax.dot_general(left, right, (((0,), (0,)), ((), ())), preferred_element_type=f32)


def folds(rows):
    return rows % 32 == 0


def fold(block):
    rows, width = block.shape
    if not folds(rows):
        return block
    whole = width // 128
    half = rows // 2
    last = jnp.concatenate([block[:half, whole * 128 :], block[half:, whole * 128 :]], axis=1)
    return jnp.concatenate([block[:, j * 128 : (j + 1) * 128] for j in range(whole)] + [last], axis=0)


def unfold(block, rows, width):
    if not folds(rows):
        return block
    whole = width // 128
    last = block[whole * rows :]
    edge = jnp.concatenate([last[:, : width - whole * 128], last[:, width - whole * 128 :]], axis=0)
    return jnp.concatenate([block[j * rows : (j + 1) * rows] for j in range(whole)] + [edge], axis=1)


def folded(rows, width):
    return (rows * width // 128, 128) if folds(rows) else (rows, width)


def params(size):
    return pltpu.CompilerParams(vmem_limit_bytes=size * mib)


def keys_kernel(piece_rows, cache_t_ref, gain_ref, keys_ref, sib_ref, piece_ref, cache_scr, gain_scr, rows_scr, sems):
    lat_width = gain_ref.shape[0]
    copies = [
        pltpu.make_async_copy(cache_t_ref, cache_scr, sems.at[0]),
        pltpu.make_async_copy(gain_ref, gain_scr, sems.at[1]),
    ]
    for copy in copies:
        copy.start()
    for copy in copies:
        copy.wait()
    raw = jnp.transpose(cache_scr[...].astype(f32))
    latent = raw[:, :lat_width]
    inverse = lax.rsqrt(jnp.mean(latent * latent, axis=1, keepdims=True) + eps_norm)
    rows_scr[:, :lat_width] = latent * inverse * gain_scr[...].astype(f32)[None, :]
    rows_scr[:, lat_width:] = raw[:, lat_width:]
    keys_ref[...] = rows_scr[...].astype(bf16)
    sib_ref[...] = fold(rows_scr[...]).astype(bf16)
    start = pl.multiple_of(lax.axis_index("head") * piece_rows, piece_rows)
    piece_ref[...] = fold(rows_scr[pl.ds(start, piece_rows), :]).astype(bf16)


def columns(ref, i, parts):
    if len(ref.shape) == 3:
        size = ref.shape[0] // parts
        return ref.at[pl.ds(i * size, size)]
    size = ref.shape[1] // parts
    return ref.at[:, pl.ds(i * size, size)]


def fetches(sources, buffers, sems, parts):
    copies = [
        [
            pltpu.make_async_copy(columns(source, i, parts), columns(buffer, i, parts), sems.at[i, a])
            for a, (source, buffer) in enumerate(zip(sources, buffers))
        ]
        for i in range(parts)
    ]
    for part in copies[:fetch_ahead]:
        for copy in part:
            copy.start()
    return copies


def arrive(copies, i):
    for copy in copies[i]:
        copy.wait()
    if i + fetch_ahead < len(copies):
        for copy in copies[i + fetch_ahead]:
            copy.start()


def query_rows_kernel(*refs):
    sources, (unused_ref, q_hbm), buffers = refs[:3], refs[3:5], refs[5:8]
    q_ref, in_sems, out_sems = refs[8:]
    nope_ref, rope_ref, w_uk_ref = buffers
    heads, nope_width, lat_width = w_uk_ref.shape
    span = nope_ref.shape[0] // 2
    rope_width = rope_ref.shape[1] // heads
    pairs = heads // 2
    copies = fetches(sources, buffers, in_sems, pairs)
    outs = []
    for i in range(pairs):
        arrive(copies, i)
        for head in (2 * i, 2 * i + 1):
            rows = slice(head * span, (head + 1) * span)
            q_lat = dot_nn(nope_ref[:, head * nope_width : (head + 1) * nope_width], w_uk_ref[head]).astype(bf16)
            for s in range(2):
                tokens = slice(s * span, (s + 1) * span)
                q_ref[s, rows, :lat_width] = q_lat[tokens]
                q_ref[s, rows, lat_width:] = rope_ref[tokens, head * rope_width : (head + 1) * rope_width]
        rows = pl.ds(2 * i * span, 2 * span)
        outs.append(pltpu.make_async_copy(q_ref.at[:, rows], q_hbm.at[:, rows], out_sems.at[i]))
        outs[i].start()
    for copy in outs:
        copy.wait()


def grad_rows_kernel(*refs):
    sources, (unused_ref, dl_hbm), buffers = refs[:3], refs[3:5], refs[5:8]
    dl_ref, delta_scr, in_sems, out_sems = refs[8:]
    grad_ref, out_ref, w_uv_ref = buffers
    heads, lat_width, value_width = w_uv_ref.shape
    span = grad_ref.shape[0] // 2
    row_count = heads * span
    pairs = heads // 2
    copies = fetches(sources, buffers, in_sems, pairs)
    outs = []
    ones = jnp.ones((8, value_width), bf16)
    delta_scr[...] = jnp.zeros(delta_scr.shape, f32)
    for i in range(pairs):
        arrive(copies, i)
        wide = slice(2 * i * value_width, 2 * (i + 1) * value_width)
        products = grad_ref[:, wide].astype(f32) * out_ref[:, wide].astype(f32)
        for p in range(2):
            head = 2 * i + p
            rows = slice(head * span, (head + 1) * span)
            d_lat = dot_nt(grad_ref[:, head * value_width : (head + 1) * value_width], w_uv_ref[head]).astype(bf16)
            for s in range(2):
                dl_ref[s, rows, :] = d_lat[s * span : (s + 1) * span]
        for s in range(2):
            tokens = slice(s * span, (s + 1) * span)
            product = jnp.concatenate([products[tokens, :value_width], products[tokens, value_width:]], axis=0)
            high = product.astype(bf16)
            low = (product - high.astype(f32)).astype(bf16)
            delta = (dot_nt(ones, high) + dot_nt(ones, low))[:1]
            row, lane = divmod(2 * i * span, lat_width)
            delta_high = delta.astype(bf16).astype(f32)
            delta_scr[s, row : row + 1, lane : lane + 2 * span] = delta_high
            delta_scr[s, 8 + row : 9 + row, lane : lane + 2 * span] = delta - delta_high
        rows = pl.ds(2 * i * span, 2 * span)
        outs.append(pltpu.make_async_copy(dl_ref.at[:, rows], dl_hbm.at[:, rows], out_sems.at[i]))
        outs[i].start()
    dl_ref[:, row_count:, :] = delta_scr[...].astype(bf16)
    rows = pl.ds(row_count, delta_rows)
    outs.append(pltpu.make_async_copy(dl_ref.at[:, rows], dl_hbm.at[:, rows], out_sems.at[pairs]))
    outs[pairs].start()
    for copy in outs:
        copy.wait()


def join_kernel(*refs):
    refs[-2][...] = jnp.concatenate([ref[...].astype(f32) for ref in refs[:-3]], axis=0).astype(bf16)


def tile_place(u, tile_count, span, lower_block):
    per_tile = key_tile // span
    upper_count = (tile_count * per_tile - 1 - lower_block) // per_tile + 1
    if u <= tile_count // 2:
        return True, u
    if u == tile_count:
        return False, 0
    is_upper = u < upper_count
    return is_upper, jnp.where(is_upper, u, tile_count - u)


def pick(is_upper, upper, lower):
    if isinstance(is_upper, bool):
        return upper if is_upper else lower
    return jnp.where(is_upper, upper, lower)


def half_of(is_upper):
    return int(is_upper) if isinstance(is_upper, bool) else is_upper.astype(jnp.int32)


def tile_rows(kt):
    if isinstance(kt, int):
        return slice(kt * key_tile, (kt + 1) * key_tile)
    return pl.ds(pl.multiple_of(kt * key_tile, key_tile), key_tile)


def attend_kernel(scale, head_count, *refs):
    span_ref, own_ref, sib_ref, own_pieces, sib_pieces, q_hbm, dl_hbm, keys_ref, ds_hbm, keep_ref, send_ref = refs[:-9]
    e_scr, dk_scr, stage, q_ref, dl_ref, ds_ref, prob_scr, sems, ds_sems = refs[-9:]
    copies = [
        pltpu.make_async_copy(hbm.at[s], ref.at[s], sems.at[i, s])
        for i, (hbm, ref) in enumerate(((q_hbm, q_ref), (dl_hbm, dl_ref)))
        for s in (1, 0)
    ]
    copies[0].start()
    half_count, row_count, cat_width = q_ref.shape
    lat_width = dl_ref.shape[2]
    tok_rows = own_ref.shape[0]
    span = tok_rows // 2
    total = keys_ref.shape[0]
    tile_count = total // key_tile
    z_count = total // tok_rows // 2
    piece_rows = tok_rows // head_count
    per_span = span // piece_rows
    me, head = lax.axis_index("ctx"), lax.axis_index("head")
    z, core = me // 2, lax.rem(me, 2)

    def place(owner, quarter):
        block = span_ref[quarter // per_span, owner]
        start = block * span + lax.rem(quarter, per_span) * piece_rows
        return pl.ds(pl.multiple_of(start, piece_rows), piece_rows)

    sib_rows = unfold(sib_ref[...], tok_rows, cat_width)
    for owner, rows in ((me, own_ref[...]), (2 * z + 1 - core, sib_rows)):
        for s in range(2):
            start = pl.multiple_of(span_ref[s, owner] * span, span)
            stage[pl.ds(start, span), :] = rows[s * span : (s + 1) * span, :].astype(stage.dtype)
    for side, ref in enumerate((own_pieces, sib_pieces)):
        rows = ref[...].astype(stage.dtype)
        size = rows.shape[0] // (z_count - 1) // head_count
        for m in range(head_count):
            for k in range(1, z_count):
                owner = 2 * (z ^ k) + lax.rem(core + side, 2)
                start = (m * (z_count - 1) + k - 1) * size
                stage[place(owner, head ^ m), :] = unfold(rows[start : start + size], piece_rows, cat_width)
    keys_ref[...] = stage[...].astype(bf16)

    my_lower, my_upper = span_ref[0, me], span_ref[1, me]
    step_shape = (key_tile, min(row_chunk, row_count))
    key_step = lax.broadcasted_iota(jnp.int32, step_shape, 0)
    row_step = lax.rem(lax.broadcasted_iota(jnp.int32, step_shape, 1), span)
    step = row_step - key_step
    places = [tile_place(u, tile_count, span, my_lower) for u in range(tile_count + 1)]
    chunks = [slice(n, n + min(row_chunk, row_count)) for n in range(0, row_count, row_chunk)]
    tops, sums = [], []
    copies[0].wait()
    for copy in copies[1:]:
        copy.start()
    for u, (is_upper, kt) in enumerate(places):
        if u == tile_count // 2 + 1:
            copies[1].wait()
        top_parts, sum_parts = [], []
        for chunk in chunks:
            scores = dot_nt(keys_ref[tile_rows(kt), :], q_ref[half_of(is_upper), chunk]) * (scale * log2_e)
            if u >= tile_count // 2:
                base = kt * key_tile - pick(is_upper, my_upper, my_lower) * span
                scores = jnp.where(step >= base, scores, neg_big)
            top = jnp.max(scores, axis=0, keepdims=True)
            weights = jnp.exp2(scores - top)
            e_scr[u, :, chunk] = weights
            top_parts.append(top)
            sum_parts.append(jnp.sum(weights, axis=0, keepdims=True))
        tops.append(jnp.concatenate(top_parts, axis=1))
        sums.append(jnp.concatenate(sum_parts, axis=1))
    row_top, row_sum = [], []
    for s in range(2):
        kept = [jnp.where(half_of(is_upper) == s, top, neg_big) for (is_upper, kt), top in zip(places, tops)]
        best = functools.reduce(jnp.maximum, kept)
        row_top.append(best)
        row_sum.append(functools.reduce(jnp.add, [jnp.exp2(top - best) * add for top, add in zip(kept, sums)]))
    factors = []
    for (is_upper, kt), top in zip(places, tops):
        best = pick(is_upper, row_top[1], row_top[0])
        factors.append(jnp.exp2(top - best) / pick(is_upper, row_sum[1], row_sum[0]))
    dk_scr[(tile_count // 2 + 1) * key_tile :, :] = jnp.zeros(
        (total - (tile_count // 2 + 1) * key_tile, cat_width), f32
    )
    copies[2].wait()
    copies[3].wait()
    deltas = []
    for s in range(2):
        parts = dl_ref[s, row_count:, :].astype(f32)
        width = min(lat_width, row_count)
        rows = [parts[j : j + 1, :width] + parts[8 + j : 9 + j, :width] for j in range(row_count // width)]
        deltas.append(jnp.concatenate(rows, axis=1))
    ds_copies = []

    def score_grads(u):
        is_upper, kt = places[u]
        half = half_of(is_upper)
        delta = pick(is_upper, deltas[1], deltas[0])
        for chunk in chunks:
            d_prob = dot_nt(keys_ref[tile_rows(kt), :lat_width], dl_ref[half, chunk])
            prob = e_scr[u, :, chunk] * factors[u][:, chunk]
            ds_ref[u, :, chunk] = (prob * scale * (d_prob - delta[:, chunk])).astype(bf16)
            prob_scr[u % 2, :, chunk] = prob.astype(bf16)
        ds_copies.append(pltpu.make_async_copy(ds_ref.at[u], ds_hbm.at[u], ds_sems.at[u]))
        ds_copies[u].start()

    def key_grads(u):
        is_upper, kt = places[u]
        half = half_of(is_upper)
        key_part = dot_nn(ds_ref[u], q_ref[half])
        latent_part = key_part[:, :lat_width] + dot_nn(prob_scr[u % 2], dl_ref[half, :row_count])
        if u <= tile_count // 2:
            dk_scr[tile_rows(kt), :lat_width] = latent_part
            dk_scr[tile_rows(kt), lat_width:] = key_part[:, lat_width:]
        else:
            dk_scr[tile_rows(kt), :lat_width] += latent_part
            dk_scr[tile_rows(kt), lat_width:] += key_part[:, lat_width:]

    score_grads(0)
    for u in range(tile_count + 1):
        if u < tile_count:
            score_grads(u + 1)
        key_grads(u)
    for side, ref in ((0, keep_ref), (1, send_ref)):
        for quarter in range(head_count):
            rows = [
                fold(dk_scr[place(2 * other + lax.rem(core + side, 2), jnp.int32(quarter)), :])
                for other in range(z_count)
            ]
            share = ref.shape[0] // head_count
            ref[quarter * share : (quarter + 1) * share, :] = jnp.concatenate(rows, axis=0).astype(bf16)
    for copy in ds_copies:
        copy.wait()


def query_kernel(
    span_ref, keys_ref, ds_hbm, w_uk_hbm, unused_ref, nope_ref, rope_ref, token_ref, dq_scr, ds_ref, w_uk_ref, sems
):
    tile_total, unused_rows, row_count = ds_ref.shape
    copies = [pltpu.make_async_copy(ds_hbm.at[u], ds_ref.at[u], sems.at[u]) for u in range(tile_total)]
    copies.append(pltpu.make_async_copy(w_uk_hbm, w_uk_ref, sems.at[tile_total]))
    for copy in copies[:tile_total]:
        copy.start()
    token_ref[...] = jnp.zeros(token_ref.shape, f32)
    tile_count = tile_total - 1
    heads, nope_width, lat_width = w_uk_ref.shape
    span = row_count // heads
    cat_width = keys_ref.shape[1]
    my_lower = span_ref[0, lax.axis_index("ctx")]
    places = [tile_place(u, tile_count, span, my_lower) for u in range(tile_total)]
    sure = tile_count // 2 + 1
    for copy in copies[:sure]:
        copy.wait()
    copies[tile_total].start()
    dq_scr[1] = dot_tn(keys_ref[: sure * key_tile, :], ds_ref[:sure].reshape(sure * key_tile, row_count))
    for copy in copies[sure:tile_total]:
        copy.wait()
    dq_scr[0] = dot_tn(keys_ref[:key_tile, :], ds_ref[tile_count])
    for u, (is_upper, kt) in enumerate(places):
        if not isinstance(is_upper, bool):
            dq_scr[half_of(is_upper)] += dot_tn(keys_ref[tile_rows(kt), :], ds_ref[u])
    copies[tile_total].wait()
    for pair in range(heads // 2):
        wide = slice(pair * 2 * span, (pair + 1) * 2 * span)
        turned = [jnp.transpose(dq_scr[s, :, wide]) for s in range(2)]
        for p in range(2):
            head = 2 * pair + p
            rows = jnp.concatenate([t[p * span : (p + 1) * span, :lat_width] for t in turned], axis=0)
            nope_ref[:, head * nope_width : (head + 1) * nope_width] = dot_nt(
                rows.astype(bf16), w_uk_ref[head]
            ).astype(bf16)
        rope = [
            jnp.concatenate([t[p * span : (p + 1) * span, lat_width:] for t in turned], axis=0) for p in range(2)
        ]
        width = 2 * (cat_width - lat_width)
        rope_ref[:, pair * width : (pair + 1) * width] = jnp.concatenate(rope, axis=1).astype(bf16)


def pair_sum_kernel(keep_ref, recv_ref, own_ref, *send_refs):
    head = lax.axis_index("head")
    share = own_ref.shape[0]

    def both(target):
        rows = pl.ds(pl.multiple_of(target * share, share), share)
        return keep_ref[rows, :].astype(f32) + recv_ref[rows, :].astype(f32)

    own_ref[...] = both(head)
    for m, ref in enumerate(send_refs, 1):
        ref[...] = both(head ^ m).astype(bf16)


def head_sum_kernel(*refs):
    z_count = refs[0].shape[0] // refs[-2].shape[0]
    head_count = len(refs) - 2 - z_count
    terms, own_ref, send_refs, total = refs[:head_count], refs[head_count + 1], refs[head_count + 2 : -1], refs[-1]
    total[...] = functools.reduce(jnp.add, [ref[...].astype(f32) for ref in terms])
    rows = own_ref.shape[0]
    z = lax.axis_index("ctx") // 2

    def share(k):
        return total[pl.ds(pl.multiple_of((z ^ k) * rows, rows), rows), :]

    own_ref[...] = share(0)
    for k, ref in enumerate(send_refs, 1):
        ref[...] = share(k).astype(bf16)


def chip_sum_kernel(*refs):
    refs[-1][...] = functools.reduce(jnp.add, [ref[...].astype(f32) for ref in refs[:-1]]).astype(bf16)


def norm_back_kernel(cache_t_ref, gain_ref, *refs):
    shares, out_ref, total = refs[:-2], refs[-2], refs[-1]
    head = lax.axis_index("head")
    rows = total.shape[0] // len(shares)
    lat_width = gain_ref.shape[0]
    for m, ref in enumerate(shares):
        total[pl.ds(pl.multiple_of((head ^ m) * rows, rows), rows), :] = unfold(
            ref[...].astype(f32), rows, total.shape[1]
        )
    values = cache_t_ref[:lat_width, :].astype(f32)
    inverse = lax.rsqrt(jnp.mean(values * values, axis=0, keepdims=True) + eps_norm)
    scaled = jnp.transpose(total[:, :lat_width] * gain_ref[...].astype(f32)[None, :])
    inner = jnp.mean(values * scaled, axis=0, keepdims=True)
    out_ref[:lat_width, :] = inverse * scaled - values * (inverse * inverse * inverse * inner)
    out_ref[lat_width:, :] = jnp.transpose(total[:, lat_width:])


def local(q_nope, q_rope, kv_cache, kv_gain, w_uk, w_uv, attn_out, d_out, span_table):
    shape = jax.ShapeDtypeStruct
    tok_rows, cat_width = kv_cache.shape
    heads, nope_width, lat_width = w_uk.shape
    value_width = w_uv.shape[2]
    rope_width = q_rope.shape[1] // heads
    span = tok_rows // 2
    row_count = span * heads
    scale = float(nope_width + rope_width) ** (-0.5)
    ctx_count, head_count = lax.axis_size("ctx"), lax.axis_size("head")
    z_count = ctx_count // 2
    total = ctx_count * tok_rows
    tile_total = total // key_tile + 1
    piece_rows = tok_rows // head_count
    cache_t = kv_cache.T
    spans = span_table.T

    def to_core(rows):
        return lax.ppermute(rows, "ctx", [(i, i ^ 1) for i in range(ctx_count)])

    def to_chip(rows, k):
        return lax.ppermute(rows, "ctx", [(i, i ^ (2 * k)) for i in range(ctx_count)])

    def to_head(rows, m):
        return lax.ppermute(rows, "head", [(j, j ^ m) for j in range(head_count)])

    keys_own, keys_out, piece = pl.pallas_call(
        functools.partial(keys_kernel, piece_rows),
        out_shape=(
            shape((tok_rows, cat_width), bf16),
            shape(folded(tok_rows, cat_width), bf16),
            shape(folded(piece_rows, cat_width), bf16),
        ),
        in_specs=[in_hbm] * 2,
        out_specs=(in_vmem,) * 3,
        scratch_shapes=[
            pltpu.VMEM((cat_width, tok_rows), bf16),
            pltpu.VMEM((lat_width,), bf16),
            pltpu.VMEM((tok_rows, cat_width), f32),
            pltpu.SemaphoreType.DMA((2,)),
        ],
        compiler_params=params(fetch_mib),
        name="keys",
    )(cache_t, kv_gain)
    keys_sib = to_core(keys_out)
    pieces = [to_chip(piece, k) for k in range(1, z_count)]
    pairs = heads // 2
    projection = pl.CostEstimate(
        flops=4 * row_count * nope_width * lat_width, bytes_accessed=6 * mib, transcendentals=0
    )

    def project(kernel, inputs, order, out_shape, scratch, name):
        return pl.pallas_call(
            kernel,
            out_shape=shape(out_shape, bf16),
            in_specs=[in_any] * 4,
            out_specs=in_any,
            scratch_shapes=[pltpu.VMEM(a.shape, bf16) for a in inputs]
            + [pltpu.VMEM(out_shape, bf16)]
            + scratch
            + [pltpu.SemaphoreType.DMA((pairs, 3)), pltpu.SemaphoreType.DMA((pairs + 1,))],
            compiler_params=params(fetch_mib),
            cost_estimate=projection,
            name=name,
        )(*inputs, order)

    def join(rows, order, name):
        return pl.pallas_call(
            join_kernel,
            out_shape=(shape((sum(r.shape[0] for r in rows), rows[0].shape[1]), bf16), shape((4096, 256), f32)),
            in_specs=[in_vmem] * len(rows) + [in_any],
            out_specs=(in_vmem, in_any),
            compiler_params=params(wide_mib),
            name=name,
        )(*rows, order)

    queries = project(
        query_rows_kernel, (q_nope, q_rope, w_uk), piece, (2, row_count, cat_width), [], "query_rows"
    )
    pieces, token = join(pieces, queries, "join_chips")
    d_latent = project(
        grad_rows_kernel,
        (d_out, attn_out, w_uv),
        token,
        (2, row_count + delta_rows, lat_width),
        [pltpu.VMEM((2, delta_rows, lat_width), f32)],
        "grad_rows",
    )
    pieces, token = join([pieces] + [to_head(pieces, m) for m in range(1, head_count)], d_latent, "join_heads")
    sib_pieces = to_core(pieces)

    piece_shape = piece.shape
    share_shape = (z_count * piece_shape[0], piece_shape[1])
    all_shape = (head_count * share_shape[0], piece_shape[1])
    keys, d_score, keep, send = pl.pallas_call(
        functools.partial(attend_kernel, scale, head_count),
        out_shape=(
            shape((total, cat_width), bf16),
            shape((tile_total, key_tile, row_count), bf16),
            shape(all_shape, bf16),
            shape(all_shape, bf16),
        ),
        in_specs=[in_smem] + [in_vmem] * 4 + [in_any] * 2,
        out_specs=(in_vmem, in_any, in_vmem, in_vmem),
        scratch_shapes=[
            pltpu.VMEM((tile_total, key_tile, row_count), f32),
            pltpu.VMEM((total, cat_width), f32),
            pltpu.VMEM((total, cat_width), bf16 if piece_rows % 16 == 0 else f32),
            pltpu.VMEM(queries.shape, bf16),
            pltpu.VMEM(d_latent.shape, bf16),
            pltpu.VMEM((tile_total, key_tile, row_count), bf16),
            pltpu.VMEM((2, key_tile, row_count), bf16),
            pltpu.SemaphoreType.DMA((2, 2)),
            pltpu.SemaphoreType.DMA((tile_total,)),
        ],
        compiler_params=params(50),
        cost_estimate=pl.CostEstimate(
            flops=2 * tile_total * key_tile * row_count * (2 * cat_width + 2 * lat_width),
            bytes_accessed=12 * mib,
            transcendentals=tile_total * key_tile * row_count,
        ),
        name="attend",
    )(spans, keys_own, keys_sib, pieces, sib_pieces, queries, d_latent)

    recv = to_core(send)
    sums = pl.pallas_call(
        pair_sum_kernel,
        out_shape=(shape(share_shape, f32),) + (shape(share_shape, bf16),) * (head_count - 1),
        in_specs=[in_vmem] * 2,
        out_specs=(in_vmem,) * head_count,
        compiler_params=params(4),
        name="pair_sum",
    )(keep, recv)
    d_q_nope, d_q_rope, token = pl.pallas_call(
        query_kernel,
        out_shape=(shape(q_nope.shape, bf16), shape(q_rope.shape, bf16), shape((8, 128), f32)),
        in_specs=[in_smem, in_vmem] + [in_any] * 3,
        out_specs=(in_vmem,) * 3,
        scratch_shapes=[
            pltpu.VMEM((2, cat_width, row_count), f32),
            pltpu.VMEM(d_score.shape, bf16),
            pltpu.VMEM(w_uk.shape, bf16),
            pltpu.SemaphoreType.DMA((tile_total + 1,)),
        ],
        compiler_params=params(query_mib),
        cost_estimate=pl.CostEstimate(
            flops=2 * tile_total * key_tile * row_count * cat_width,
            bytes_accessed=8 * mib,
            transcendentals=0,
        ),
        name="query_grads",
    )(spans, keys, d_score, w_uk, sums[0])
    terms = [sums[0]] + [to_head(rows, m) for m, rows in enumerate(sums[1:], 1)]
    sums = pl.pallas_call(
        head_sum_kernel,
        out_shape=(shape(piece_shape, f32),) + (shape(piece_shape, bf16),) * (z_count - 1),
        in_specs=[in_vmem] * head_count + [in_any],
        out_specs=(in_vmem,) * z_count,
        scratch_shapes=[pltpu.VMEM(share_shape, f32)],
        compiler_params=params(4),
        name="head_sum",
    )(*terms, token)
    terms = [sums[0]] + [to_chip(rows, k) for k, rows in enumerate(sums[1:], 1)]
    share = pl.pallas_call(
        chip_sum_kernel,
        out_shape=shape(piece_shape, bf16),
        in_specs=[in_vmem] * z_count,
        out_specs=in_vmem,
        compiler_params=params(4),
        name="chip_sum",
    )(*terms)
    shares = [share] + [to_head(share, m) for m in range(1, head_count)]
    d_cache_t = pl.pallas_call(
        norm_back_kernel,
        out_shape=shape((cat_width, tok_rows), f32),
        in_specs=[in_vmem] * (2 + head_count),
        out_specs=in_vmem,
        scratch_shapes=[pltpu.VMEM((tok_rows, cat_width), f32)],
        compiler_params=params(8),
        name="norm_back",
    )(cache_t, kv_gain, *shares)
    return (d_q_nope, d_q_rope, d_cache_t.T)


def solution(mesh):
    in_specs = (
        P("ctx", "head"),
        P("ctx", "head"),
        P("ctx", None),
        P(),
        P("head", None, None),
        P("head", None, None),
        P("ctx", "head"),
        P("ctx", "head"),
        P(),
    )
    out_specs = (P("ctx", "head"), P("ctx", "head"), P("ctx", None))
    return jax.shard_map(local, mesh=mesh, in_specs=in_specs, out_specs=out_specs, check_vma=False)
```

```python
import functools

import jax
import jax.numpy as jnp
from jax import lax
from jax.experimental import pallas as pl
from jax.experimental.pallas import tpu as pltpu
from jax.sharding import PartitionSpec as P

neg_big = -1e30
eps_norm = 1e-06
log2_e = 1.4426950408889634
key_tile = 128
mib = 1024 * 1024
piece_mib = 53.8
query_mib = 16
attend_mib = 36
project_mib = 12
window_flops = 8 * 10**9
delta_rows = 16
row_chunk = 256
f32 = jnp.float32
bf16 = jnp.bfloat16
in_vmem = pl.BlockSpec(memory_space=pltpu.VMEM)
in_hbm = pl.BlockSpec(memory_space=pltpu.HBM)
in_any = pl.BlockSpec(memory_space=pl.ANY)
in_smem = pl.BlockSpec(memory_space=pltpu.SMEM)


def dot_nn(left, right):
    return lax.dot_general(left, right, (((1,), (0,)), ((), ())), preferred_element_type=f32)


def dot_nt(left, right):
    return lax.dot_general(left, right, (((1,), (1,)), ((), ())), preferred_element_type=f32)


def dot_tn(left, right):
    return lax.dot_general(left, right, (((0,), (0,)), ((), ())), preferred_element_type=f32)


def fold(block, on):
    if not on:
        return block
    rows, width = block.shape
    whole = width // 128
    half = rows // 2
    last = jnp.concatenate([block[:half, whole * 128 :], block[half:, whole * 128 :]], axis=1)
    return jnp.concatenate([block[:, j * 128 : (j + 1) * 128] for j in range(whole)] + [last], axis=0)


def unfold(block, width, on):
    if not on:
        return block
    rows = block.shape[0] * 128 // width
    whole = width // 128
    last = block[whole * rows :]
    edge = jnp.concatenate([last[:, : width - whole * 128], last[:, width - whole * 128 :]], axis=0)
    return jnp.concatenate([block[j * rows : (j + 1) * rows] for j in range(whole)] + [edge], axis=1)


def folded(rows, width, on):
    return (rows * width // 128, 128) if on else (rows, width)


def params(size):
    return pltpu.CompilerParams(vmem_limit_bytes=int(size * mib))


def piece_kernel(cache_t_hbm, piece_ref, cache_scr, rows_scr, sem):
    copy = pltpu.make_async_copy(cache_t_hbm, cache_scr, sem)
    copy.start()
    copy.wait()
    rows_scr[...] = jnp.transpose(cache_scr[...].astype(f32))
    rows = rows_scr.shape[0] // lax.axis_size("head")
    start = pl.multiple_of(lax.axis_index("head") * rows, rows)
    piece_ref[...] = fold(rows_scr[pl.ds(start, rows), :], rows % 32 == 0).astype(bf16)


def normalised(rows, gain):
    width = gain.shape[1]
    latent = rows[:, :width]
    inverse = lax.rsqrt(jnp.mean(latent * latent, axis=1, keepdims=True) + eps_norm)
    return jnp.concatenate([latent * inverse * gain, rows[:, width:]], axis=1)


def own_kernel(on, cache_t_ref, gain_ref, out_ref):
    rows = jnp.transpose(cache_t_ref[...].astype(f32))
    out_ref[...] = fold(normalised(rows, gain_ref[...].astype(f32)[None, :]), on).astype(bf16)


def join_chips_kernel(on, width, gain_ref, *refs):
    gain = gain_ref[...].astype(f32)[None, :]
    rows = jnp.concatenate([unfold(ref[...].astype(f32), width, on) for ref in refs[:-1]], axis=0)
    rows = normalised(rows, gain)
    size = rows.shape[0] // (len(refs) - 1)
    parts = [fold(rows[i * size : (i + 1) * size], on) for i in range(len(refs) - 1)]
    refs[-1][...] = jnp.concatenate(parts, axis=0).astype(bf16)


def project_kernel(
    factor, nope_ref, rope_ref, w_uk_ref, grad_ref, out_ref, w_uv_ref, unused_ref, q_ref, dl_ref, delta_scr
):
    heads, lat_width, value_width = w_uv_ref.shape
    nope_width = w_uk_ref.shape[1]
    span = grad_ref.shape[0] // 2
    rope_width = rope_ref.shape[1] // heads
    row_count = heads * span
    pairs = heads // 2
    ones = jnp.ones((8, value_width), bf16)
    for i in range(pairs):
        rope = (rope_ref[:, 2 * i * rope_width : 2 * (i + 1) * rope_width].astype(f32) * factor).astype(bf16)
        wide = slice(2 * i * value_width, 2 * (i + 1) * value_width)
        products = grad_ref[:, wide].astype(f32) * out_ref[:, wide].astype(f32)
        for p in range(2):
            head = 2 * i + p
            rows = slice(head * span, (head + 1) * span)
            q_lat = dot_nn(nope_ref[:, head * nope_width : (head + 1) * nope_width], w_uk_ref[head])
            q_lat = (q_lat * factor).astype(bf16)
            d_lat = dot_nt(grad_ref[:, head * value_width : (head + 1) * value_width], w_uv_ref[head]).astype(bf16)
            for s in range(2):
                tokens = slice(s * span, (s + 1) * span)
                q_ref[s, rows, :lat_width] = q_lat[tokens]
                q_ref[s, rows, lat_width:] = rope[tokens, p * rope_width : (p + 1) * rope_width]
                dl_ref[s, rows, :] = d_lat[tokens]
        for s in range(2):
            tokens = slice(s * span, (s + 1) * span)
            product = jnp.concatenate([products[tokens, :value_width], products[tokens, value_width:]], axis=0)
            high = product.astype(bf16)
            low = (product - high.astype(f32)).astype(bf16)
            delta_scr[i, s] = dot_nt(ones, high) + dot_nt(ones, low)

    per_row = min(lat_width // (2 * span), pairs)
    for s in range(2):
        rows = []
        for start in range(0, pairs, per_row):
            rows.append(jnp.concatenate([delta_scr[i, s, :1] for i in range(start, start + per_row)], axis=1))
        width = rows[0].shape[1]
        full = jnp.concatenate(rows + [jnp.zeros((8 - len(rows), width), f32)], axis=0)
        high = full.astype(bf16).astype(f32)
        both = jnp.concatenate([high, full - high], axis=0)
        if width < lat_width:
            both = jnp.concatenate([both, jnp.zeros((delta_rows, lat_width - width), f32)], axis=1)
        dl_ref[s, row_count:, :] = both.astype(bf16)


def join_kernel(*refs):
    if any(ref.shape[0] % 16 for ref in refs):
        refs[-1][...] = jnp.concatenate([ref[...].astype(f32) for ref in refs[:-1]], axis=0).astype(bf16)
        return
    start = 0
    for ref in refs[:-1]:
        size = ref.shape[0]
        refs[-1][start : start + size, :] = ref[...]
        start += size


def tile_groups(tile_count):
    pairs = [(u, u + 2) for u in range(0, tile_count // 2, 2)]
    return pairs + [(u, u + 1) for u in range(tile_count // 2, tile_count + 1)]


def tile_place(u, tile_count, span, lower_block):
    per_tile = key_tile // span
    upper_count = (tile_count * per_tile - 1 - lower_block) // per_tile + 1
    if u <= tile_count // 2:
        return True, u
    if u == tile_count:
        return False, 0
    is_upper = u < upper_count
    return is_upper, jnp.where(is_upper, u, tile_count - u)


def pick(is_upper, upper, lower):
    if isinstance(is_upper, bool):
        return upper if is_upper else lower
    return jnp.where(is_upper, upper, lower)


def half_of(is_upper):
    return int(is_upper) if isinstance(is_upper, bool) else is_upper.astype(jnp.int32)


def tile_rows(kt, count=1):
    if isinstance(kt, int):
        return slice(kt * key_tile, (kt + count) * key_tile)
    return pl.ds(pl.multiple_of(kt * key_tile, key_tile), key_tile)


def attend_kernel(head_count, *refs):
    span_ref, own_pieces, sib_pieces, q_ref, dl_ref, keys_ref, ds_ref, keep_ref, send_ref = refs[:-5]
    e_scr, score_part, prob_part, prob_scr, raw = refs[-5:]
    half_count, row_count, cat_width = q_ref.shape
    lat_width = dl_ref.shape[2]
    total = keys_ref.shape[0]
    tile_count = total // key_tile
    z_count = lax.axis_size("ctx") // 2
    tok_rows = total // z_count // 2
    span = tok_rows // 2
    piece_rows = tok_rows // head_count
    per_span = span // piece_rows
    me, head = lax.axis_index("ctx"), lax.axis_index("head")
    z, core = me // 2, lax.rem(me, 2)
    on = piece_rows % 32 == 0
    own_size = folded(tok_rows, cat_width, on)[0]
    piece_size = folded(piece_rows, cat_width, on)[0]

    def place(owner, quarter):
        block = span_ref[quarter // per_span, owner]
        start = block * span + lax.rem(quarter, per_span) * piece_rows
        return pl.ds(pl.multiple_of(start, piece_rows), piece_rows)

    stage = keys_ref if piece_rows % 16 == 0 else raw
    for side, ref in enumerate((own_pieces, sib_pieces)):
        source = ref if piece_rows % 16 == 0 else ref[...].astype(f32)
        rows = unfold(source[:own_size, :], cat_width, on)
        for s in range(2):
            start = pl.multiple_of(span_ref[s, 2 * z + lax.rem(core + side, 2)] * span, span)
            stage[pl.ds(start, span), :] = rows[s * span : (s + 1) * span, :]
        start = own_size
        for m in range(head_count):
            for k in range(1, z_count):
                owner = 2 * (z ^ k) + lax.rem(core + side, 2)
                stage[place(owner, head ^ m), :] = unfold(source[start : start + piece_size, :], cat_width, on)
                start += piece_size
    if stage is raw:
        keys_ref[...] = raw[...].astype(bf16)

    my_lower, my_upper = span_ref[0, me], span_ref[1, me]
    chunks = [slice(n, n + min(row_chunk, row_count)) for n in range(0, row_count, row_chunk)]
    groups = tile_groups(tile_count)
    counts = [last - first for first, last in groups]
    tiles = [slice(first * key_tile, last * key_tile) for first, last in groups]
    places = [tile_place(first, tile_count, span, my_lower) for first, last in groups]
    work = [(g, chunk) for g in range(len(groups)) for chunk in chunks]
    step_shape = (key_tile, min(row_chunk, row_count))
    key_step = lax.broadcasted_iota(jnp.int32, step_shape, 0)
    row_step = lax.rem(lax.broadcasted_iota(jnp.int32, step_shape, 1), span)
    step = row_step - key_step

    def score_dot(u, chunk):
        is_upper, kt = places[u]
        return dot_nt(keys_ref[tile_rows(kt, counts[u]), :], q_ref[half_of(is_upper), chunk])

    top_parts, sum_parts = {}, {}
    ahead = score_dot(*work[0])
    for i, (u, chunk) in enumerate(work):
        scores = ahead
        if i + 1 < len(work):
            ahead = score_dot(*work[i + 1])
        is_upper, kt = places[u]
        if groups[u][0] >= tile_count // 2:
            base = kt * key_tile - pick(is_upper, my_upper, my_lower) * span
            scores = jnp.where(step >= base, scores, neg_big)
        top = jnp.max(scores, axis=0, keepdims=True)
        weights = jnp.exp2(scores - top)
        e_scr[tiles[u], chunk] = weights
        top_parts.setdefault(u, []).append(top)
        sum_parts.setdefault(u, []).append(jnp.sum(weights, axis=0, keepdims=True))
    tops = [jnp.concatenate(top_parts[u], axis=1) for u in range(len(groups))]
    sums = [jnp.concatenate(sum_parts[u], axis=1) for u in range(len(groups))]

    def prob_dot(u, chunk):
        is_upper, kt = places[u]
        return dot_nt(keys_ref[tile_rows(kt, counts[u]), :lat_width], dl_ref[half_of(is_upper), chunk])

    ahead = prob_dot(*work[0])
    row_top, row_sum = [], []
    for s in range(2):
        kept = [jnp.where(half_of(is_upper) == s, top, neg_big) for (is_upper, kt), top in zip(places, tops)]
        best = functools.reduce(jnp.maximum, kept)
        row_top.append(best)
        row_sum.append(functools.reduce(jnp.add, [jnp.exp2(top - best) * add for top, add in zip(kept, sums)]))
    inverse = [1.0 / part for part in row_sum]
    factors = []
    for (is_upper, kt), top in zip(places, tops):
        best = pick(is_upper, row_top[1], row_top[0])
        factors.append(jnp.exp2(top - best) * pick(is_upper, inverse[1], inverse[0]))
    deltas = []
    for s in range(2):
        parts = dl_ref[s, row_count:, :].astype(f32)
        width = min(lat_width, row_count)
        rows = [parts[j : j + 1, :width] + parts[8 + j : 9 + j, :width] for j in range(row_count // width)]
        deltas.append(jnp.concatenate(rows, axis=1))
    sure = (tile_count // 2 + 1) * key_tile
    score_part[sure:, :] = jnp.zeros((total - sure, cat_width), f32)
    prob_part[sure:, :] = jnp.zeros((total - sure, lat_width), f32)

    def key_grads(u, source, target, rhs, first, last):
        is_upper, kt = places[u]
        part = dot_nn(source[...], rhs[half_of(is_upper), :row_count, first:last])
        if groups[u][0] <= tile_count // 2:
            target[tile_rows(kt, counts[u]), first:last] = part
        else:
            target[tile_rows(kt, counts[u]), first:last] += part

    def key_steps(u):
        widths = [(first, min(first + 256, cat_width)) for first in range(0, cat_width, 256)]
        steps = []
        for first, last in widths:
            steps.append(functools.partial(key_grads, u, ds_ref.at[tiles[u]], score_part, q_ref, first, last))
            if last <= lat_width:
                steps.append(functools.partial(key_grads, u, prob_scr.at[u % 2, : counts[u] * key_tile], prob_part, dl_ref, first, last))
        return steps

    pending = []
    for i, (u, chunk) in enumerate(work):
        d_prob = ahead
        if i + 1 < len(work):
            ahead = prob_dot(*work[i + 1])
        left = len(chunks) - i % len(chunks)
        for j in range(-(-len(pending) // left)):
            pending.pop(0)()
        is_upper, kt = places[u]
        delta = pick(is_upper, deltas[1], deltas[0])
        prob = e_scr[tiles[u], chunk] * factors[u][:, chunk]
        ds_ref[tiles[u], chunk] = (prob * (d_prob - delta[:, chunk])).astype(bf16)
        prob_scr[u % 2, : counts[u] * key_tile, chunk] = prob.astype(bf16)
        if left == 1:
            pending = key_steps(u)
    for key_step in pending:
        key_step()

    for side, ref in ((0, keep_ref), (1, send_ref)):
        for quarter in range(head_count):
            rows = []
            for other in range(z_count):
                here = place(2 * other + lax.rem(core + side, 2), jnp.int32(quarter))
                block = score_part[here, :] * (1.0 / log2_e)
                latent = block[:, :lat_width] + prob_part[here, :]
                rows.append(fold(jnp.concatenate([latent, block[:, lat_width:]], axis=1), on))
            size = z_count * piece_size
            ref[quarter * size : (quarter + 1) * size, :] = jnp.concatenate(rows, axis=0).astype(bf16)


def query_kernel(
    scale, span_ref, keys_ref, ds_ref, w_uk_ref, nope_ref, rope_ref, dq_scr
):
    tile_total, row_count = ds_ref.shape[0] // key_tile, ds_ref.shape[1]
    tile_count = tile_total - 1
    heads, nope_width, lat_width = w_uk_ref.shape
    span = row_count // heads
    cat_width = keys_ref.shape[1]
    my_lower = span_ref[0, lax.axis_index("ctx")]
    places = [tile_place(u, tile_count, span, my_lower) for u in range(tile_total)]
    sure = tile_count // 2 + 1
    dq_scr[1] = dot_tn(keys_ref[: sure * key_tile, :], ds_ref[: sure * key_tile, :])
    dq_scr[0] = dot_tn(keys_ref[:key_tile, :], ds_ref[tile_count * key_tile :, :])
    for u, (is_upper, kt) in enumerate(places):
        if not isinstance(is_upper, bool):
            dq_scr[half_of(is_upper)] += dot_tn(keys_ref[tile_rows(kt), :], ds_ref[tile_rows(u), :])
    for pair in range(heads // 2):
        wide = slice(pair * 2 * span, (pair + 1) * 2 * span)
        turned = [jnp.transpose(dq_scr[s, :, wide]) * scale for s in range(2)]
        for p in range(2):
            head = 2 * pair + p
            rows = jnp.concatenate([t[p * span : (p + 1) * span, :lat_width] for t in turned], axis=0)
            nope_ref[:, head * nope_width : (head + 1) * nope_width] = dot_nt(
                rows.astype(bf16), w_uk_ref[head]
            ).astype(bf16)
        rope = [
            jnp.concatenate([t[p * span : (p + 1) * span, lat_width:] for t in turned], axis=0) for p in range(2)
        ]
        width = 2 * (cat_width - lat_width)
        rope_ref[:, pair * width : (pair + 1) * width] = jnp.concatenate(rope, axis=1).astype(bf16)


def pair_sum_kernel(keep_ref, recv_ref, own_ref, *send_refs):
    head = lax.axis_index("head")
    share = own_ref.shape[0]

    def both(target):
        rows = pl.ds(pl.multiple_of(target * share, share), share)
        return keep_ref[rows, :].astype(f32) + recv_ref[rows, :].astype(f32)

    own_ref[...] = both(head)
    for m, ref in zip(range(len(send_refs), 0, -1), send_refs):
        ref[...] = both(head ^ m).astype(bf16)


def head_sum_kernel(*refs):
    z_count = refs[0].shape[0] // refs[-2].shape[0]
    head_count = len(refs) - 1 - z_count
    terms, own_ref, send_refs, total = refs[:head_count], refs[head_count], refs[head_count + 1 : -1], refs[-1]
    total[...] = functools.reduce(jnp.add, [ref[...].astype(f32) for ref in terms])
    rows = own_ref.shape[0]
    z = lax.axis_index("ctx") // 2

    def share(k):
        return total[pl.ds(pl.multiple_of((z ^ k) * rows, rows), rows), :]

    own_ref[...] = share(0)
    for k, ref in zip(range(len(send_refs), 0, -1), send_refs):
        ref[...] = share(k).astype(bf16)


def chip_sum_kernel(*refs):
    refs[-1][...] = functools.reduce(jnp.add, [ref[...].astype(f32) for ref in refs[:-1]]).astype(bf16)


def norm_back_kernel(cache_t_ref, gain_ref, *refs):
    shares, out_ref, total = refs[:-2], refs[-2], refs[-1]
    head = lax.axis_index("head")
    rows = total.shape[0] // len(shares)
    lat_width = gain_ref.shape[0]
    for m, ref in enumerate(shares):
        total[pl.ds(pl.multiple_of((head ^ m) * rows, rows), rows), :] = unfold(
            ref[...].astype(f32), total.shape[1], rows % 32 == 0
        )
    values = cache_t_ref[:lat_width, :].astype(f32)
    inverse = lax.rsqrt(jnp.mean(values * values, axis=0, keepdims=True) + eps_norm)
    scaled = jnp.transpose(total[:, :lat_width] * gain_ref[...].astype(f32)[None, :])
    inner = jnp.mean(values * scaled, axis=0, keepdims=True)
    out_ref[:lat_width, :] = inverse * scaled - values * (inverse * inverse * inverse * inner)
    out_ref[lat_width:, :] = jnp.transpose(total[:, lat_width:])


def local(q_nope, q_rope, kv_cache, kv_gain, w_uk, w_uv, attn_out, d_out, span_table):
    shape = jax.ShapeDtypeStruct
    tok_rows, cat_width = kv_cache.shape
    heads, nope_width, lat_width = w_uk.shape
    value_width = w_uv.shape[2]
    rope_width = q_rope.shape[1] // heads
    span = tok_rows // 2
    row_count = span * heads
    scale = float(nope_width + rope_width) ** (-0.5)
    ctx_count, head_count = lax.axis_size("ctx"), lax.axis_size("head")
    z_count = ctx_count // 2
    total = ctx_count * tok_rows
    tile_total = total // key_tile + 1
    piece_rows = tok_rows // head_count
    cache_t = kv_cache.T
    spans = span_table.T

    def to_core(rows):
        return lax.ppermute(rows, "ctx", [(i, i ^ 1) for i in range(ctx_count)])

    def to_chip(rows, k):
        return lax.ppermute(rows, "ctx", [(i, i ^ (2 * k)) for i in range(ctx_count)])

    def to_head(rows, m):
        return lax.ppermute(rows, "head", [(j, j ^ m) for j in range(head_count)])

    on = piece_rows % 32 == 0
    piece = pl.pallas_call(
        piece_kernel,
        out_shape=shape(folded(piece_rows, cat_width, on), bf16),
        in_specs=[in_any],
        out_specs=in_vmem,
        scratch_shapes=[
            pltpu.VMEM((cat_width, tok_rows), bf16),
            pltpu.VMEM((tok_rows, cat_width), f32),
            pltpu.SemaphoreType.DMA,
        ],
        compiler_params=params(piece_mib),
        name="piece",
    )(cache_t)
    pieces = [to_chip(piece, k) for k in range(1, z_count)]
    keys_own = pl.pallas_call(
        functools.partial(own_kernel, on),
        out_shape=shape(folded(tok_rows, cat_width, on), bf16),
        in_specs=[in_vmem] * 2,
        out_specs=in_vmem,
        compiler_params=params(8),
        cost_estimate=pl.CostEstimate(flops=window_flops, bytes_accessed=mib, transcendentals=0),
        name="own_keys",
    )(cache_t, kv_gain)
    *pieces, keys_own = lax.optimization_barrier((*pieces, keys_own))
    pieces = pl.pallas_call(
        functools.partial(join_chips_kernel, on, cat_width),
        out_shape=shape(((z_count - 1) * piece.shape[0], piece.shape[1]), bf16),
        in_specs=[in_vmem] * z_count,
        out_specs=in_vmem,
        compiler_params=params(8),
        name="join_chips",
    )(kv_gain, *pieces)

    def join(rows, name):
        return pl.pallas_call(
            join_kernel,
            out_shape=shape((sum(r.shape[0] for r in rows), rows[0].shape[1]), bf16),
            in_specs=[in_vmem] * len(rows),
            out_specs=in_vmem,
            compiler_params=params(4),
            name=name,
        )(*rows)

    queries, d_latent = pl.pallas_call(
        functools.partial(project_kernel, scale * log2_e),
        out_shape=(shape((2, row_count, cat_width), bf16), shape((2, row_count + delta_rows, lat_width), bf16)),
        in_specs=[in_vmem] * 6 + [in_any],
        out_specs=(in_vmem,) * 2,
        scratch_shapes=[pltpu.VMEM((heads // 2, 2, 8, 2 * span), f32)],
        compiler_params=params(project_mib),
        cost_estimate=pl.CostEstimate(
            flops=8 * row_count * nope_width * lat_width, bytes_accessed=12 * mib, transcendentals=0
        ),
        name="project",
    )(q_nope, q_rope, w_uk, d_out, attn_out, w_uv, pieces)
    pieces = [pieces] + [to_head(pieces, m) for m in range(1, head_count)]
    *pieces, queries, d_latent = lax.optimization_barrier((*pieces, queries, d_latent))
    pieces = join([keys_own] + pieces, "join_heads")
    sib_pieces = to_core(pieces)

    piece_shape = piece.shape
    share_shape = (z_count * piece_shape[0], piece_shape[1])
    all_shape = (head_count * share_shape[0], piece_shape[1])
    keys, d_score, keep, send = pl.pallas_call(
        functools.partial(attend_kernel, head_count),
        out_shape=(
            shape((total, cat_width), bf16),
            shape((tile_total * key_tile, row_count), bf16),
            shape(all_shape, bf16),
            shape(all_shape, bf16),
        ),
        in_specs=[in_smem] + [in_vmem] * 4,
        out_specs=(in_vmem,) * 4,
        scratch_shapes=[
            pltpu.VMEM((tile_total * key_tile, row_count), f32),
            pltpu.VMEM((total, cat_width), f32),
            pltpu.VMEM((total, lat_width), f32),
            pltpu.VMEM((2, 2 * key_tile, row_count), bf16),
            pltpu.VMEM((8, 128) if piece_rows % 16 == 0 else (total, cat_width), f32),
        ],
        compiler_params=params(attend_mib if total <= 2048 else 56),
        cost_estimate=pl.CostEstimate(
            flops=2 * tile_total * key_tile * row_count * (2 * cat_width + 2 * lat_width),
            bytes_accessed=12 * mib,
            transcendentals=tile_total * key_tile * row_count,
        ),
        name="attend",
    )(spans, pieces, sib_pieces, queries, d_latent)

    recv = to_core(send)
    sums = pl.pallas_call(
        pair_sum_kernel,
        out_shape=(shape(share_shape, f32),) + (shape(share_shape, bf16),) * (head_count - 1),
        in_specs=[in_vmem] * 2,
        out_specs=(in_vmem,) * head_count,
        compiler_params=params(4),
        name="pair_sum",
    )(keep, recv)
    *sums, d_score = lax.optimization_barrier((*sums, d_score))
    d_q_nope, d_q_rope = pl.pallas_call(
        functools.partial(query_kernel, scale),
        out_shape=(shape(q_nope.shape, bf16), shape(q_rope.shape, bf16)),
        in_specs=[in_smem] + [in_vmem] * 3,
        out_specs=(in_vmem,) * 2,
        scratch_shapes=[pltpu.VMEM((2, cat_width, row_count), f32)],
        compiler_params=params(query_mib),
        cost_estimate=pl.CostEstimate(
            flops=2 * tile_total * key_tile * row_count * cat_width,
            bytes_accessed=8 * mib,
            transcendentals=0,
        ),
        name="query_grads",
    )(spans, keys, d_score, w_uk)
    terms = [sums[0]] + [to_head(rows, m) for m, rows in zip(range(head_count - 1, 0, -1), sums[1:])]
    *terms, d_q_nope, d_q_rope = lax.optimization_barrier((*terms, d_q_nope, d_q_rope))
    sums = pl.pallas_call(
        head_sum_kernel,
        out_shape=(shape(piece_shape, f32),) + (shape(piece_shape, bf16),) * (z_count - 1),
        in_specs=[in_vmem] * head_count,
        out_specs=(in_vmem,) * z_count,
        scratch_shapes=[pltpu.VMEM(share_shape, f32)],
        compiler_params=params(4),
        name="head_sum",
    )(*terms)
    terms = [sums[0]] + [to_chip(rows, k) for k, rows in zip(range(z_count - 1, 0, -1), sums[1:])]
    share = pl.pallas_call(
        chip_sum_kernel,
        out_shape=shape(piece_shape, bf16),
        in_specs=[in_vmem] * z_count,
        out_specs=in_vmem,
        compiler_params=params(4),
        name="chip_sum",
    )(*terms)
    shares = [share] + [to_head(share, m) for m in range(1, head_count)]
    d_cache_t = pl.pallas_call(
        norm_back_kernel,
        out_shape=shape((cat_width, tok_rows), f32),
        in_specs=[in_vmem] * (2 + head_count),
        out_specs=in_vmem,
        scratch_shapes=[pltpu.VMEM((tok_rows, cat_width), f32)],
        compiler_params=params(8),
        name="norm_back",
    )(cache_t, kv_gain, *shares)
    return (d_q_nope, d_q_rope, d_cache_t.T)


def solution(mesh):
    in_specs = (
        P("ctx", "head"),
        P("ctx", "head"),
        P("ctx", None),
        P(),
        P("head", None, None),
        P("head", None, None),
        P("ctx", "head"),
        P("ctx", "head"),
        P(),
    )
    out_specs = (P("ctx", "head"), P("ctx", "head"), P("ctx", None))
    return jax.shard_map(local, mesh=mesh, in_specs=in_specs, out_specs=out_specs, check_vma=False)
```

```python
import functools

import jax
import jax.numpy as jnp
from jax import lax
from jax.experimental import pallas as pl
from jax.experimental.pallas import tpu as pltpu
from jax.sharding import PartitionSpec as P

neg_big = -1e30
eps_norm = 1e-06
log2_e = 1.4426950408889634
key_tile = 256
mib = 1024 * 1024
piece_mib = 53.8
query_mib = 16
attend_mib = 28
project_mib = 12
window_flops = 8 * 10**9
delta_rows = 16
row_chunk = 256
f32 = jnp.float32
bf16 = jnp.bfloat16
in_vmem = pl.BlockSpec(memory_space=pltpu.VMEM)
in_hbm = pl.BlockSpec(memory_space=pltpu.HBM)
in_any = pl.BlockSpec(memory_space=pl.ANY)
in_smem = pl.BlockSpec(memory_space=pltpu.SMEM)


def dot_nn(left, right):
    return lax.dot_general(left, right, (((1,), (0,)), ((), ())), preferred_element_type=f32)


def dot_nt(left, right):
    return lax.dot_general(left, right, (((1,), (1,)), ((), ())), preferred_element_type=f32)


def dot_tn(left, right):
    return lax.dot_general(left, right, (((0,), (0,)), ((), ())), preferred_element_type=f32)


def fold(block, on):
    if not on:
        return block
    rows, width = block.shape
    whole = width // 128
    half = rows // 2
    last = jnp.concatenate([block[:half, whole * 128 :], block[half:, whole * 128 :]], axis=1)
    return jnp.concatenate([block[:, j * 128 : (j + 1) * 128] for j in range(whole)] + [last], axis=0)


def unfold(block, width, on):
    if not on:
        return block
    rows = block.shape[0] * 128 // width
    whole = width // 128
    last = block[whole * rows :]
    edge = jnp.concatenate([last[:, : width - whole * 128], last[:, width - whole * 128 :]], axis=0)
    return jnp.concatenate([block[j * rows : (j + 1) * rows] for j in range(whole)] + [edge], axis=1)


def folded(rows, width, on):
    return (rows * width // 128, 128) if on else (rows, width)


def params(size):
    return pltpu.CompilerParams(vmem_limit_bytes=int(size * mib))


def piece_kernel(cache_t_hbm, piece_ref, cache_scr, rows_scr, sem):
    copy = pltpu.make_async_copy(cache_t_hbm, cache_scr, sem)
    copy.start()
    copy.wait()
    rows_scr[...] = jnp.transpose(cache_scr[...].astype(f32))
    rows = rows_scr.shape[0] // lax.axis_size("head")
    start = pl.multiple_of(lax.axis_index("head") * rows, rows)
    piece_ref[...] = fold(rows_scr[pl.ds(start, rows), :], rows % 32 == 0).astype(bf16)


def normalised(rows, gain):
    width = gain.shape[1]
    latent = rows[:, :width]
    inverse = lax.rsqrt(jnp.mean(latent * latent, axis=1, keepdims=True) + eps_norm)
    return jnp.concatenate([latent * inverse * gain, rows[:, width:]], axis=1)


def own_kernel(on, cache_t_ref, gain_ref, out_ref):
    rows = jnp.transpose(cache_t_ref[...].astype(f32))
    out_ref[...] = fold(normalised(rows, gain_ref[...].astype(f32)[None, :]), on).astype(bf16)


def join_chips_kernel(on, width, gain_ref, own_ref, *refs):
    refs, pieces_ref, first_ref = refs[:-2], refs[-2], refs[-1]
    gain = gain_ref[...].astype(f32)[None, :]
    rows = jnp.concatenate([unfold(ref[...].astype(f32), width, on) for ref in refs], axis=0)
    rows = normalised(rows, gain)
    size = rows.shape[0] // len(refs)
    parts = [fold(rows[i * size : (i + 1) * size], on) for i in range(len(refs))]
    pieces = jnp.concatenate(parts, axis=0).astype(bf16)
    pieces_ref[...] = pieces
    first_ref[: own_ref.shape[0], :] = own_ref[...]
    first_ref[own_ref.shape[0] :, :] = pieces


def project_kernel(
    factor, nope_ref, rope_ref, w_uk_ref, grad_ref, out_ref, w_uv_ref, unused_ref, q_ref, dl_ref, delta_scr
):
    heads, lat_width, value_width = w_uv_ref.shape
    nope_width = w_uk_ref.shape[1]
    span = grad_ref.shape[0] // 2
    rope_width = rope_ref.shape[1] // heads
    row_count = heads * span
    pairs = heads // 2
    ones = jnp.ones((8, value_width), bf16)
    for i in range(pairs):
        rope = (rope_ref[:, 2 * i * rope_width : 2 * (i + 1) * rope_width].astype(f32) * factor).astype(bf16)
        wide = slice(2 * i * value_width, 2 * (i + 1) * value_width)
        products = grad_ref[:, wide].astype(f32) * out_ref[:, wide].astype(f32)
        for p in range(2):
            head = 2 * i + p
            rows = slice(head * span, (head + 1) * span)
            q_lat = dot_nn(nope_ref[:, head * nope_width : (head + 1) * nope_width], w_uk_ref[head])
            q_lat = (q_lat * factor).astype(bf16)
            d_lat = dot_nt(grad_ref[:, head * value_width : (head + 1) * value_width], w_uv_ref[head]).astype(bf16)
            for s in range(2):
                tokens = slice(s * span, (s + 1) * span)
                q_ref[s, rows, :lat_width] = q_lat[tokens]
                q_ref[s, rows, lat_width:] = rope[tokens, p * rope_width : (p + 1) * rope_width]
                dl_ref[s, rows, :] = d_lat[tokens]
        for s in range(2):
            tokens = slice(s * span, (s + 1) * span)
            product = jnp.concatenate([products[tokens, :value_width], products[tokens, value_width:]], axis=0)
            high = product.astype(bf16)
            low = (product - high.astype(f32)).astype(bf16)
            delta_scr[i, s] = dot_nt(ones, high) + dot_nt(ones, low)

    per_row = min(lat_width // (2 * span), pairs)
    for s in range(2):
        rows = []
        for start in range(0, pairs, per_row):
            rows.append(jnp.concatenate([delta_scr[i, s, :1] for i in range(start, start + per_row)], axis=1))
        width = rows[0].shape[1]
        full = jnp.concatenate(rows + [jnp.zeros((8 - len(rows), width), f32)], axis=0)
        high = full.astype(bf16).astype(f32)
        both = jnp.concatenate([high, full - high], axis=0)
        if width < lat_width:
            both = jnp.concatenate([both, jnp.zeros((delta_rows, lat_width - width), f32)], axis=1)
        dl_ref[s, row_count:, :] = both.astype(bf16)


def join_kernel(*refs):
    if any(ref.shape[0] % 16 for ref in refs):
        refs[-1][...] = jnp.concatenate([ref[...].astype(f32) for ref in refs[:-1]], axis=0).astype(bf16)
        return
    start = 0
    for ref in refs[:-1]:
        size = ref.shape[0]
        refs[-1][start : start + size, :] = ref[...]
        start += size


def tile_groups(tile_count):
    return [(u, u + 1) for u in range(tile_count + 1)]


def tile_place(u, tile_count, span, lower_block):
    per_tile = key_tile // span
    upper_count = (tile_count * per_tile - 1 - lower_block) // per_tile + 1
    if u <= tile_count // 2:
        return True, u
    if u == tile_count:
        return False, 0
    is_upper = u < upper_count
    return is_upper, jnp.where(is_upper, u, tile_count - u)


def pick(is_upper, upper, lower):
    if isinstance(is_upper, bool):
        return upper if is_upper else lower
    return jnp.where(is_upper, upper, lower)


def half_of(is_upper):
    return int(is_upper) if isinstance(is_upper, bool) else is_upper.astype(jnp.int32)


def tile_rows(kt, count=1):
    if isinstance(kt, int):
        return slice(kt * key_tile, (kt + count) * key_tile)
    return pl.ds(pl.multiple_of(kt * key_tile, key_tile), key_tile)


def attend_kernel(head_count, *refs):
    span_ref, own_first, own_later, sib_first, sib_later, q_ref, dl_ref = refs[:7]
    keys_ref, ds_ref, send_ref, score_part, prob_part, e_scr, prob_scr, raw = refs[7:]
    half_count, row_count, cat_width = q_ref.shape
    lat_width = dl_ref.shape[2]
    total = keys_ref.shape[0]
    tile_count = total // key_tile
    z_count = lax.axis_size("ctx") // 2
    tok_rows = total // z_count // 2
    span = tok_rows // 2
    piece_rows = tok_rows // head_count
    per_span = span // piece_rows
    me, head = lax.axis_index("ctx"), lax.axis_index("head")
    z, core = me // 2, lax.rem(me, 2)
    on = piece_rows % 32 == 0
    own_size = folded(tok_rows, cat_width, on)[0]
    piece_size = folded(piece_rows, cat_width, on)[0]

    def place(owner, quarter):
        block = span_ref[quarter // per_span, owner]
        start = block * span + lax.rem(quarter, per_span) * piece_rows
        return pl.ds(pl.multiple_of(start, piece_rows), piece_rows)

    stage = keys_ref if piece_rows % 16 == 0 else raw
    for side, parts in enumerate(((own_first, own_later), (sib_first, sib_later))):
        first, later = parts if piece_rows % 16 == 0 else [ref[...].astype(f32) for ref in parts]
        rows = unfold(first[:own_size, :], cat_width, on)
        for s in range(2):
            start = pl.multiple_of(span_ref[s, 2 * z + lax.rem(core + side, 2)] * span, span)
            stage[pl.ds(start, span), :] = rows[s * span : (s + 1) * span, :]
        for m in range(head_count):
            source = later if m else first
            start = (m - 1) * (z_count - 1) * piece_size if m else own_size
            for k in range(1, z_count):
                owner = 2 * (z ^ k) + lax.rem(core + side, 2)
                stage[place(owner, head ^ m), :] = unfold(source[start : start + piece_size, :], cat_width, on)
                start += piece_size
    if stage is raw:
        keys_ref[...] = raw[...].astype(bf16)

    my_lower, my_upper = span_ref[0, me], span_ref[1, me]
    chunks = [slice(n, n + min(row_chunk, row_count)) for n in range(0, row_count, row_chunk)]
    groups = tile_groups(tile_count)
    counts = [last - first for first, last in groups]
    tiles = [slice(first * key_tile, last * key_tile) for first, last in groups]
    places = [tile_place(first, tile_count, span, my_lower) for first, last in groups]
    work = [(g, chunk) for g in range(len(groups)) for chunk in chunks]
    step_shape = (key_tile, min(row_chunk, row_count))
    key_step = lax.broadcasted_iota(jnp.int32, step_shape, 0)
    row_step = lax.rem(lax.broadcasted_iota(jnp.int32, step_shape, 1), span)
    step = row_step - key_step

    def score_dot(u, chunk):
        is_upper, kt = places[u]
        return dot_nt(keys_ref[tile_rows(kt, counts[u]), :], q_ref[half_of(is_upper), chunk])

    top_parts, sum_parts = {}, {}
    ahead = score_dot(*work[0])
    for i, (u, chunk) in enumerate(work):
        scores = ahead
        if i + 1 < len(work):
            ahead = score_dot(*work[i + 1])
        is_upper, kt = places[u]
        if groups[u][0] >= tile_count // 2:
            base = kt * key_tile - pick(is_upper, my_upper, my_lower) * span
            scores = jnp.where(step >= base, scores, neg_big)
        top = jnp.max(scores, axis=0, keepdims=True)
        weights = jnp.exp2(scores - top)
        e_scr[tiles[u], chunk] = weights
        top_parts.setdefault(u, []).append(top)
        sum_parts.setdefault(u, []).append(jnp.sum(weights, axis=0, keepdims=True))
    tops = [jnp.concatenate(top_parts[u], axis=1) for u in range(len(groups))]
    sums = [jnp.concatenate(sum_parts[u], axis=1) for u in range(len(groups))]

    def prob_dot(u, chunk):
        is_upper, kt = places[u]
        return dot_nt(keys_ref[tile_rows(kt, counts[u]), :lat_width], dl_ref[half_of(is_upper), chunk])

    ahead = prob_dot(*work[0])
    row_top, row_sum = [], []
    for s in range(2):
        kept = [jnp.where(half_of(is_upper) == s, top, neg_big) for (is_upper, kt), top in zip(places, tops)]
        best = functools.reduce(jnp.maximum, kept)
        row_top.append(best)
        row_sum.append(functools.reduce(jnp.add, [jnp.exp2(top - best) * add for top, add in zip(kept, sums)]))
    inverse = [1.0 / part for part in row_sum]
    factors = []
    for (is_upper, kt), top in zip(places, tops):
        best = pick(is_upper, row_top[1], row_top[0])
        factors.append(jnp.exp2(top - best) * pick(is_upper, inverse[1], inverse[0]))
    deltas = []
    for s in range(2):
        parts = dl_ref[s, row_count:, :].astype(f32)
        width = min(lat_width, row_count)
        rows = [parts[j : j + 1, :width] + parts[8 + j : 9 + j, :width] for j in range(row_count // width)]
        deltas.append(jnp.concatenate(rows, axis=1))
    sure = (tile_count // 2 + 1) * key_tile
    score_part[sure:, :] = jnp.zeros((total - sure, cat_width), f32)
    prob_part[sure:, :] = jnp.zeros((total - sure, lat_width), f32)

    def key_grads(u, source, target, rhs, first, last):
        is_upper, kt = places[u]
        part = dot_nn(source[...], rhs[half_of(is_upper), :row_count, first:last])
        if groups[u][0] <= tile_count // 2:
            target[tile_rows(kt, counts[u]), first:last] = part
        else:
            target[tile_rows(kt, counts[u]), first:last] += part

    def key_steps(u):
        widths = [(first, min(first + 256, cat_width)) for first in range(0, cat_width, 256)]
        steps = []
        for first, last in widths:
            steps.append(functools.partial(key_grads, u, ds_ref.at[tiles[u]], score_part, q_ref, first, last))
            if last <= lat_width:
                steps.append(functools.partial(key_grads, u, prob_scr.at[u % 2, : counts[u] * key_tile], prob_part, dl_ref, first, last))
        return steps

    pending = []
    for i, (u, chunk) in enumerate(work):
        d_prob = ahead
        if i + 1 < len(work):
            ahead = prob_dot(*work[i + 1])
        left = len(chunks) - i % len(chunks)
        for j in range(-(-len(pending) // left)):
            pending.pop(0)()
        is_upper, kt = places[u]
        delta = pick(is_upper, deltas[1], deltas[0])
        prob = e_scr[tiles[u], chunk] * factors[u][:, chunk]
        ds_ref[tiles[u], chunk] = (prob * (d_prob - delta[:, chunk])).astype(bf16)
        prob_scr[u % 2, : counts[u] * key_tile, chunk] = prob.astype(bf16)
        if left == 1:
            pending = key_steps(u)
    for key_step in pending:
        key_step()

    pack(1, head_count, span_ref, score_part, prob_part, send_ref)


def pack(side, head_count, span_ref, score_part, prob_part, out_ref):
    total, cat_width = score_part.shape
    lat_width = prob_part.shape[1]
    z_count = lax.axis_size("ctx") // 2
    piece_rows = total // z_count // 2 // head_count
    span = total // z_count // 4
    per_span = span // piece_rows
    on = piece_rows % 32 == 0
    size = z_count * folded(piece_rows, cat_width, on)[0]
    owner_core = lax.rem(lax.axis_index("ctx") + side, 2)
    for quarter in range(head_count):
        rows = []
        for other in range(z_count):
            block = span_ref[quarter // per_span, 2 * other + owner_core]
            start = block * span + quarter % per_span * piece_rows
            here = pl.ds(pl.multiple_of(start, piece_rows), piece_rows)
            terms = score_part[here, :] * (1.0 / log2_e)
            latent = terms[:, :lat_width] + prob_part[here, :]
            rows.append(fold(jnp.concatenate([latent, terms[:, lat_width:]], axis=1), on))
        out_ref[quarter * size : (quarter + 1) * size, :] = jnp.concatenate(rows, axis=0).astype(bf16)


def query_kernel(
    scale, span_ref, keys_ref, ds_ref, w_uk_ref, nope_ref, rope_ref, dq_scr
):
    tile_total, row_count = ds_ref.shape[0] // key_tile, ds_ref.shape[1]
    tile_count = tile_total - 1
    heads, nope_width, lat_width = w_uk_ref.shape
    span = row_count // heads
    cat_width = keys_ref.shape[1]
    my_lower = span_ref[0, lax.axis_index("ctx")]
    places = [tile_place(u, tile_count, span, my_lower) for u in range(tile_total)]
    sure = tile_count // 2 + 1
    dq_scr[1] = dot_tn(keys_ref[: sure * key_tile, :], ds_ref[: sure * key_tile, :])
    dq_scr[0] = dot_tn(keys_ref[:key_tile, :], ds_ref[tile_count * key_tile :, :])
    for u, (is_upper, kt) in enumerate(places):
        if not isinstance(is_upper, bool):
            dq_scr[half_of(is_upper)] += dot_tn(keys_ref[tile_rows(kt), :], ds_ref[tile_rows(u), :])
    for pair in range(heads // 2):
        wide = slice(pair * 2 * span, (pair + 1) * 2 * span)
        turned = [jnp.transpose(dq_scr[s, :, wide]) * scale for s in range(2)]
        for p in range(2):
            head = 2 * pair + p
            rows = jnp.concatenate([t[p * span : (p + 1) * span, :lat_width] for t in turned], axis=0)
            nope_ref[:, head * nope_width : (head + 1) * nope_width] = dot_nt(
                rows.astype(bf16), w_uk_ref[head]
            ).astype(bf16)
        rope = [
            jnp.concatenate([t[p * span : (p + 1) * span, lat_width:] for t in turned], axis=0) for p in range(2)
        ]
        width = 2 * (cat_width - lat_width)
        rope_ref[:, pair * width : (pair + 1) * width] = jnp.concatenate(rope, axis=1).astype(bf16)


def pair_sum_kernel(keep_ref, recv_ref, own_ref, *send_refs):
    head = lax.axis_index("head")
    share = own_ref.shape[0]

    def both(target):
        rows = pl.ds(pl.multiple_of(target * share, share), share)
        return keep_ref[rows, :].astype(f32) + recv_ref[rows, :].astype(f32)

    own_ref[...] = both(head)
    for m, ref in zip(range(len(send_refs), 0, -1), send_refs):
        ref[...] = both(head ^ m).astype(bf16)


def head_sum_kernel(*refs):
    z_count = refs[0].shape[0] // refs[-2].shape[0]
    head_count = len(refs) - 1 - z_count
    terms, own_ref, send_refs, total = refs[:head_count], refs[head_count], refs[head_count + 1 : -1], refs[-1]
    total[...] = functools.reduce(jnp.add, [ref[...].astype(f32) for ref in terms])
    rows = own_ref.shape[0]
    z = lax.axis_index("ctx") // 2

    def share(k):
        return total[pl.ds(pl.multiple_of((z ^ k) * rows, rows), rows), :]

    own_ref[...] = share(0)
    for k, ref in zip(range(len(send_refs), 0, -1), send_refs):
        ref[...] = share(k).astype(bf16)


def chip_sum_kernel(*refs):
    refs[-1][...] = functools.reduce(jnp.add, [ref[...].astype(f32) for ref in refs[:-1]]).astype(bf16)


def norm_back_kernel(cache_t_ref, gain_ref, *refs):
    shares, (out_hbm, total, out_ref, sems) = refs[:-4], refs[-4:]
    head = lax.axis_index("head")
    rows = total.shape[0] // len(shares)
    lat_width = gain_ref.shape[0]
    for m, ref in enumerate(shares):
        total[pl.ds(pl.multiple_of((head ^ m) * rows, rows), rows), :] = unfold(
            ref[...].astype(f32), total.shape[1], rows % 32 == 0
        )
    blocks = [slice(j, min(j + 128, total.shape[1])) for j in range(0, total.shape[1], 128)]
    copies = [pltpu.make_async_copy(out_ref.at[b], out_hbm.at[b], sems.at[j]) for j, b in enumerate(blocks)]
    values = cache_t_ref[:lat_width, :].astype(f32)
    inverse = lax.rsqrt(jnp.mean(values * values, axis=0, keepdims=True) + eps_norm)
    out_ref[lat_width:, :] = jnp.transpose(total[:, lat_width:])
    copies[-1].start()
    scaled = jnp.transpose(total[:, :lat_width] * gain_ref[...].astype(f32)[None, :])
    inner = jnp.mean(values * scaled, axis=0, keepdims=True)
    factor = inverse * inverse * inverse * inner
    for block, copy in zip(blocks[:-1], copies):
        out_ref[block, :] = inverse * scaled[block] - values[block] * factor
        copy.start()
    for copy in copies:
        copy.wait()


def local(q_nope, q_rope, kv_cache, kv_gain, w_uk, w_uv, attn_out, d_out, span_table):
    shape = jax.ShapeDtypeStruct
    tok_rows, cat_width = kv_cache.shape
    heads, nope_width, lat_width = w_uk.shape
    value_width = w_uv.shape[2]
    rope_width = q_rope.shape[1] // heads
    span = tok_rows // 2
    row_count = span * heads
    scale = float(nope_width + rope_width) ** (-0.5)
    ctx_count, head_count = lax.axis_size("ctx"), lax.axis_size("head")
    z_count = ctx_count // 2
    total = ctx_count * tok_rows
    tile_total = total // key_tile + 1
    piece_rows = tok_rows // head_count
    cache_t = kv_cache.T
    spans = span_table.T

    def to_core(rows):
        return lax.ppermute(rows, "ctx", [(i, i ^ 1) for i in range(ctx_count)])

    def to_chip(rows, k):
        return lax.ppermute(rows, "ctx", [(i, i ^ (2 * k)) for i in range(ctx_count)])

    def to_head(rows, m):
        return lax.ppermute(rows, "head", [(j, j ^ m) for j in range(head_count)])

    on = piece_rows % 32 == 0
    piece = pl.pallas_call(
        piece_kernel,
        out_shape=shape(folded(piece_rows, cat_width, on), bf16),
        in_specs=[in_any],
        out_specs=in_vmem,
        scratch_shapes=[
            pltpu.VMEM((cat_width, tok_rows), bf16),
            pltpu.VMEM((tok_rows, cat_width), f32),
            pltpu.SemaphoreType.DMA,
        ],
        compiler_params=params(piece_mib),
        name="piece",
    )(cache_t)
    pieces = [to_chip(piece, k) for k in range(1, z_count)]
    keys_own = pl.pallas_call(
        functools.partial(own_kernel, on),
        out_shape=shape(folded(tok_rows, cat_width, on), bf16),
        in_specs=[in_vmem] * 2,
        out_specs=in_vmem,
        compiler_params=params(8),
        cost_estimate=pl.CostEstimate(flops=window_flops, bytes_accessed=mib, transcendentals=0),
        name="own_keys",
    )(cache_t, kv_gain)
    *pieces, keys_own = lax.optimization_barrier((*pieces, keys_own))
    piece_total = (z_count - 1) * piece.shape[0]
    pieces, first = pl.pallas_call(
        functools.partial(join_chips_kernel, on, cat_width),
        out_shape=(
            shape((piece_total, piece.shape[1]), bf16),
            shape((keys_own.shape[0] + piece_total, piece.shape[1]), bf16),
        ),
        in_specs=[in_vmem] * (z_count + 1),
        out_specs=(in_vmem,) * 2,
        compiler_params=params(8),
        name="join_chips",
    )(kv_gain, keys_own, *pieces)
    sib_first = to_core(first)

    def join(rows, name):
        return pl.pallas_call(
            join_kernel,
            out_shape=shape((sum(r.shape[0] for r in rows), rows[0].shape[1]), bf16),
            in_specs=[in_vmem] * len(rows),
            out_specs=in_vmem,
            compiler_params=params(4),
            name=name,
        )(*rows)

    queries, d_latent = pl.pallas_call(
        functools.partial(project_kernel, scale * log2_e),
        out_shape=(shape((2, row_count, cat_width), bf16), shape((2, row_count + delta_rows, lat_width), bf16)),
        in_specs=[in_vmem] * 6 + [in_any],
        out_specs=(in_vmem,) * 2,
        scratch_shapes=[pltpu.VMEM((heads // 2, 2, 8, 2 * span), f32)],
        compiler_params=params(project_mib),
        cost_estimate=pl.CostEstimate(
            flops=8 * row_count * nope_width * lat_width, bytes_accessed=12 * mib, transcendentals=0
        ),
        name="project",
    )(q_nope, q_rope, w_uk, d_out, attn_out, w_uv, pieces)
    pieces = [to_head(pieces, m) for m in range(1, head_count)]
    *pieces, sib_first, queries, d_latent = lax.optimization_barrier((*pieces, sib_first, queries, d_latent))
    later = join(pieces, "join_heads")
    sib_later = to_core(later)

    piece_shape = piece.shape
    share_shape = (z_count * piece_shape[0], piece_shape[1])
    all_shape = (head_count * share_shape[0], piece_shape[1])
    keys, d_score, send, score_part, prob_part = pl.pallas_call(
        functools.partial(attend_kernel, head_count),
        out_shape=(
            shape((total, cat_width), bf16),
            shape((tile_total * key_tile, row_count), bf16),
            shape(all_shape, bf16),
            shape((total, cat_width), f32),
            shape((total, lat_width), f32),
        ),
        in_specs=[in_smem] + [in_vmem] * 6,
        out_specs=(in_vmem,) * 5,
        scratch_shapes=[
            pltpu.VMEM((tile_total * key_tile, row_count), f32),
            pltpu.VMEM((2, key_tile, row_count), bf16),
            pltpu.VMEM((8, 128) if piece_rows % 16 == 0 else (total, cat_width), f32),
        ],
        compiler_params=params(attend_mib if total <= 2048 else 56),
        cost_estimate=pl.CostEstimate(
            flops=2 * tile_total * key_tile * row_count * (2 * cat_width + 2 * lat_width),
            bytes_accessed=12 * mib,
            transcendentals=tile_total * key_tile * row_count,
        ),
        name="attend",
    )(spans, first, later, sib_first, sib_later, queries, d_latent)

    recv = to_core(send)
    keep = pl.pallas_call(
        functools.partial(pack, 0, head_count),
        out_shape=shape(all_shape, bf16),
        in_specs=[in_smem] + [in_vmem] * 2,
        out_specs=in_vmem,
        compiler_params=params(6),
        name="pack_keep",
    )(spans, score_part, prob_part)
    sums = pl.pallas_call(
        pair_sum_kernel,
        out_shape=(shape(share_shape, f32),) + (shape(share_shape, bf16),) * (head_count - 1),
        in_specs=[in_vmem] * 2,
        out_specs=(in_vmem,) * head_count,
        compiler_params=params(4),
        name="pair_sum",
    )(keep, recv)
    *sums, d_score = lax.optimization_barrier((*sums, d_score))
    d_q_nope, d_q_rope = pl.pallas_call(
        functools.partial(query_kernel, scale),
        out_shape=(shape(q_nope.shape, bf16), shape(q_rope.shape, bf16)),
        in_specs=[in_smem] + [in_vmem] * 3,
        out_specs=(in_vmem,) * 2,
        scratch_shapes=[pltpu.VMEM((2, cat_width, row_count), f32)],
        compiler_params=params(query_mib),
        cost_estimate=pl.CostEstimate(
            flops=2 * tile_total * key_tile * row_count * cat_width,
            bytes_accessed=8 * mib,
            transcendentals=0,
        ),
        name="query_grads",
    )(spans, keys, d_score, w_uk)
    terms = [sums[0]] + [to_head(rows, m) for m, rows in zip(range(head_count - 1, 0, -1), sums[1:])]
    *terms, d_q_nope, d_q_rope = lax.optimization_barrier((*terms, d_q_nope, d_q_rope))
    sums = pl.pallas_call(
        head_sum_kernel,
        out_shape=(shape(piece_shape, f32),) + (shape(piece_shape, bf16),) * (z_count - 1),
        in_specs=[in_vmem] * head_count,
        out_specs=(in_vmem,) * z_count,
        scratch_shapes=[pltpu.VMEM(share_shape, f32)],
        compiler_params=params(4),
        name="head_sum",
    )(*terms)
    terms = [sums[0]] + [to_chip(rows, k) for k, rows in zip(range(z_count - 1, 0, -1), sums[1:])]
    share = pl.pallas_call(
        chip_sum_kernel,
        out_shape=shape(piece_shape, bf16),
        in_specs=[in_vmem] * z_count,
        out_specs=in_vmem,
        compiler_params=params(4),
        name="chip_sum",
    )(*terms)
    shares = [share] + [to_head(share, m) for m in range(1, head_count)]
    d_cache_t = pl.pallas_call(
        norm_back_kernel,
        out_shape=shape((cat_width, tok_rows), f32),
        in_specs=[in_vmem] * (2 + head_count),
        out_specs=in_any,
        scratch_shapes=[
            pltpu.VMEM((tok_rows, cat_width), f32),
            pltpu.VMEM((cat_width, tok_rows), f32),
            pltpu.SemaphoreType.DMA((-(-cat_width // 128),)),
        ],
        compiler_params=params(8),
        name="norm_back",
    )(cache_t, kv_gain, *shares)
    return (d_q_nope, d_q_rope, d_cache_t.T)


def solution(mesh):
    in_specs = (
        P("ctx", "head"),
        P("ctx", "head"),
        P("ctx", None),
        P(),
        P("head", None, None),
        P("head", None, None),
        P("ctx", "head"),
        P("ctx", "head"),
        P(),
    )
    out_specs = (P("ctx", "head"), P("ctx", "head"), P("ctx", None))
    return jax.shard_map(local, mesh=mesh, in_specs=in_specs, out_specs=out_specs, check_vma=False)
```

```python
import functools

import jax
import jax.numpy as jnp
from jax import lax
from jax.experimental import pallas as pl
from jax.experimental.pallas import tpu as pltpu
from jax.sharding import PartitionSpec as P

neg_big = -1e30
eps_norm = 1e-06
log2_e = 1.4426950408889634
key_tile = 256
mib = 1024 * 1024
piece_mib = 53.8
query_mib = 16
attend_mib = 28
project_mib = 12
window_flops = 8 * 10**9
delta_rows = 16
row_chunk = 256
f32 = jnp.float32
bf16 = jnp.bfloat16
in_vmem = pl.BlockSpec(memory_space=pltpu.VMEM)
in_hbm = pl.BlockSpec(memory_space=pltpu.HBM)
in_any = pl.BlockSpec(memory_space=pl.ANY)
in_smem = pl.BlockSpec(memory_space=pltpu.SMEM)


def dot_nn(left, right):
    return lax.dot_general(left, right, (((1,), (0,)), ((), ())), preferred_element_type=f32)


def dot_nt(left, right):
    return lax.dot_general(left, right, (((1,), (1,)), ((), ())), preferred_element_type=f32)


def dot_tn(left, right):
    return lax.dot_general(left, right, (((0,), (0,)), ((), ())), preferred_element_type=f32)


def fold(block, on):
    if not on:
        return block
    rows, width = block.shape
    whole = width // 128
    half = rows // 2
    last = jnp.concatenate([block[:half, whole * 128 :], block[half:, whole * 128 :]], axis=1)
    return jnp.concatenate([block[:, j * 128 : (j + 1) * 128] for j in range(whole)] + [last], axis=0)


def unfold(block, width, on):
    if not on:
        return block
    rows = block.shape[0] * 128 // width
    whole = width // 128
    last = block[whole * rows :]
    edge = jnp.concatenate([last[:, : width - whole * 128], last[:, width - whole * 128 :]], axis=0)
    return jnp.concatenate([block[j * rows : (j + 1) * rows] for j in range(whole)] + [edge], axis=1)


def folded(rows, width, on):
    return (rows * width // 128, 128) if on else (rows, width)


def params(size):
    return pltpu.CompilerParams(vmem_limit_bytes=int(size * mib))


def piece_kernel(cache_t_hbm, piece_ref, cache_scr, rows_scr, sem):
    copy = pltpu.make_async_copy(cache_t_hbm, cache_scr, sem)
    copy.start()
    copy.wait()
    rows_scr[...] = jnp.transpose(cache_scr[...].astype(f32))
    rows = rows_scr.shape[0] // lax.axis_size("head")
    start = pl.multiple_of(lax.axis_index("head") * rows, rows)
    piece_ref[...] = fold(rows_scr[pl.ds(start, rows), :], rows % 32 == 0).astype(bf16)


def normalised(rows, gain):
    width = gain.shape[1]
    latent = rows[:, :width]
    inverse = lax.rsqrt(jnp.mean(latent * latent, axis=1, keepdims=True) + eps_norm)
    return jnp.concatenate([latent * inverse * gain, rows[:, width:]], axis=1)


def own_kernel(on, cache_t_ref, gain_ref, out_ref):
    rows = jnp.transpose(cache_t_ref[...].astype(f32))
    out_ref[...] = fold(normalised(rows, gain_ref[...].astype(f32)[None, :]), on).astype(bf16)


def join_chips_kernel(on, width, gain_ref, *refs):
    gain = gain_ref[...].astype(f32)[None, :]
    rows = jnp.concatenate([unfold(ref[...].astype(f32), width, on) for ref in refs[:-1]], axis=0)
    rows = normalised(rows, gain)
    size = rows.shape[0] // (len(refs) - 1)
    parts = [fold(rows[i * size : (i + 1) * size], on) for i in range(len(refs) - 1)]
    refs[-1][...] = jnp.concatenate(parts, axis=0).astype(bf16)


def project_kernel(
    factor, nope_ref, rope_ref, w_uk_ref, grad_ref, out_ref, w_uv_ref, unused_ref, q_ref, dl_ref, delta_scr
):
    heads, lat_width, value_width = w_uv_ref.shape
    nope_width = w_uk_ref.shape[1]
    span = grad_ref.shape[0] // 2
    rope_width = rope_ref.shape[1] // heads
    row_count = heads * span
    pairs = heads // 2
    ones = jnp.ones((8, value_width), bf16)
    for i in range(pairs):
        rope = (rope_ref[:, 2 * i * rope_width : 2 * (i + 1) * rope_width].astype(f32) * factor).astype(bf16)
        wide = slice(2 * i * value_width, 2 * (i + 1) * value_width)
        products = grad_ref[:, wide].astype(f32) * out_ref[:, wide].astype(f32)
        for p in range(2):
            head = 2 * i + p
            rows = slice(head * span, (head + 1) * span)
            q_lat = dot_nn(nope_ref[:, head * nope_width : (head + 1) * nope_width], w_uk_ref[head])
            q_lat = (q_lat * factor).astype(bf16)
            d_lat = dot_nt(grad_ref[:, head * value_width : (head + 1) * value_width], w_uv_ref[head]).astype(bf16)
            for s in range(2):
                tokens = slice(s * span, (s + 1) * span)
                q_ref[s, rows, :lat_width] = q_lat[tokens]
                q_ref[s, rows, lat_width:] = rope[tokens, p * rope_width : (p + 1) * rope_width]
                dl_ref[s, rows, :] = d_lat[tokens]
        for s in range(2):
            tokens = slice(s * span, (s + 1) * span)
            product = jnp.concatenate([products[tokens, :value_width], products[tokens, value_width:]], axis=0)
            high = product.astype(bf16)
            low = (product - high.astype(f32)).astype(bf16)
            delta_scr[i, s] = dot_nt(ones, high) + dot_nt(ones, low)

    per_row = min(lat_width // (2 * span), pairs)
    for s in range(2):
        rows = []
        for start in range(0, pairs, per_row):
            rows.append(jnp.concatenate([delta_scr[i, s, :1] for i in range(start, start + per_row)], axis=1))
        width = rows[0].shape[1]
        full = jnp.concatenate(rows + [jnp.zeros((8 - len(rows), width), f32)], axis=0)
        high = full.astype(bf16).astype(f32)
        both = jnp.concatenate([high, full - high], axis=0)
        if width < lat_width:
            both = jnp.concatenate([both, jnp.zeros((delta_rows, lat_width - width), f32)], axis=1)
        dl_ref[s, row_count:, :] = both.astype(bf16)


def join_kernel(*refs):
    if any(ref.shape[0] % 16 for ref in refs):
        refs[-1][...] = jnp.concatenate([ref[...].astype(f32) for ref in refs[:-1]], axis=0).astype(bf16)
        return
    start = 0
    for ref in refs[:-1]:
        size = ref.shape[0]
        refs[-1][start : start + size, :] = ref[...]
        start += size


def tile_groups(tile_count):
    return [(u, u + 1) for u in range(tile_count + 1)]


def tile_place(u, tile_count, span, lower_block):
    per_tile = key_tile // span
    upper_count = (tile_count * per_tile - 1 - lower_block) // per_tile + 1
    if u <= tile_count // 2:
        return True, u
    if u == tile_count:
        return False, 0
    is_upper = u < upper_count
    return is_upper, jnp.where(is_upper, u, tile_count - u)


def pick(is_upper, upper, lower):
    if isinstance(is_upper, bool):
        return upper if is_upper else lower
    return jnp.where(is_upper, upper, lower)


def half_of(is_upper):
    return int(is_upper) if isinstance(is_upper, bool) else is_upper.astype(jnp.int32)


def tile_rows(kt, count=1):
    if isinstance(kt, int):
        return slice(kt * key_tile, (kt + count) * key_tile)
    return pl.ds(pl.multiple_of(kt * key_tile, key_tile), key_tile)


def place_rows(head_count, side, span_ref, source, keys_ref):
    total, cat_width = keys_ref.shape
    z_count = lax.axis_size("ctx") // 2
    span = total // z_count // 4
    piece_rows = 2 * span // head_count
    per_span = span // piece_rows
    on = piece_rows % 32 == 0
    start = folded(2 * span, cat_width, on)[0]
    size = folded(piece_rows, cat_width, on)[0]
    me, head = lax.axis_index("ctx"), lax.axis_index("head")
    source = source if piece_rows % 16 == 0 else source[...].astype(f32)
    rows = unfold(source[:start, :], cat_width, on).astype(keys_ref.dtype)
    for s in range(2):
        row = pl.multiple_of(span_ref[s, me ^ side] * span, span)
        keys_ref[pl.ds(row, span), :] = rows[s * span : (s + 1) * span, :]
    for m in range(head_count):
        quarter = head ^ m
        for k in range(1, z_count):
            owner = 2 * (me // 2 ^ k) + lax.rem(me + side, 2)
            row = span_ref[quarter // per_span, owner] * span + lax.rem(quarter, per_span) * piece_rows
            rows = unfold(source[start : start + size, :], cat_width, on)
            keys_ref[pl.ds(pl.multiple_of(row, piece_rows), piece_rows), :] = rows.astype(keys_ref.dtype)
            start += size


def attend_kernel(head_count, *refs):
    span_ref, sib_pieces, placed_ref, q_ref, dl_ref = refs[:5]
    keys_ref, ds_ref, send_ref, score_part, prob_part, e_scr, prob_scr = refs[5:]
    half_count, row_count, cat_width = q_ref.shape
    lat_width = dl_ref.shape[2]
    total = keys_ref.shape[0]
    tile_count = total // key_tile
    span = total // lax.axis_size("ctx") // 2
    me = lax.axis_index("ctx")
    if placed_ref.dtype == keys_ref.dtype:
        place_rows(head_count, 1, span_ref, sib_pieces, keys_ref)
    else:
        place_rows(head_count, 1, span_ref, sib_pieces, placed_ref)
        keys_ref[...] = placed_ref[...].astype(bf16)

    my_lower, my_upper = span_ref[0, me], span_ref[1, me]
    chunks = [slice(n, n + min(row_chunk, row_count)) for n in range(0, row_count, row_chunk)]
    groups = tile_groups(tile_count)
    counts = [last - first for first, last in groups]
    tiles = [slice(first * key_tile, last * key_tile) for first, last in groups]
    places = [tile_place(first, tile_count, span, my_lower) for first, last in groups]
    work = [(g, chunk) for g in range(len(groups)) for chunk in chunks]
    step_shape = (key_tile, min(row_chunk, row_count))
    key_step = lax.broadcasted_iota(jnp.int32, step_shape, 0)
    row_step = lax.rem(lax.broadcasted_iota(jnp.int32, step_shape, 1), span)
    step = row_step - key_step

    def score_dot(u, chunk):
        is_upper, kt = places[u]
        return dot_nt(keys_ref[tile_rows(kt, counts[u]), :], q_ref[half_of(is_upper), chunk])

    top_parts, sum_parts = {}, {}
    ahead = score_dot(*work[0])
    for i, (u, chunk) in enumerate(work):
        scores = ahead
        if i + 1 < len(work):
            ahead = score_dot(*work[i + 1])
        is_upper, kt = places[u]
        if groups[u][0] >= tile_count // 2:
            base = kt * key_tile - pick(is_upper, my_upper, my_lower) * span
            scores = jnp.where(step >= base, scores, neg_big)
        top = jnp.max(scores, axis=0, keepdims=True)
        weights = jnp.exp2(scores - top)
        e_scr[tiles[u], chunk] = weights
        top_parts.setdefault(u, []).append(top)
        sum_parts.setdefault(u, []).append(jnp.sum(weights, axis=0, keepdims=True))
    tops = [jnp.concatenate(top_parts[u], axis=1) for u in range(len(groups))]
    sums = [jnp.concatenate(sum_parts[u], axis=1) for u in range(len(groups))]

    def prob_dot(u, chunk):
        is_upper, kt = places[u]
        return dot_nt(keys_ref[tile_rows(kt, counts[u]), :lat_width], dl_ref[half_of(is_upper), chunk])

    ahead = prob_dot(*work[0])
    row_top, row_sum = [], []
    for s in range(2):
        kept = [jnp.where(half_of(is_upper) == s, top, neg_big) for (is_upper, kt), top in zip(places, tops)]
        best = functools.reduce(jnp.maximum, kept)
        row_top.append(best)
        row_sum.append(functools.reduce(jnp.add, [jnp.exp2(top - best) * add for top, add in zip(kept, sums)]))
    inverse = [1.0 / part for part in row_sum]
    factors = []
    for (is_upper, kt), top in zip(places, tops):
        best = pick(is_upper, row_top[1], row_top[0])
        factors.append(jnp.exp2(top - best) * pick(is_upper, inverse[1], inverse[0]))
    deltas = []
    for s in range(2):
        parts = dl_ref[s, row_count:, :].astype(f32)
        width = min(lat_width, row_count)
        rows = [parts[j : j + 1, :width] + parts[8 + j : 9 + j, :width] for j in range(row_count // width)]
        deltas.append(jnp.concatenate(rows, axis=1))
    sure = (tile_count // 2 + 1) * key_tile
    score_part[sure:, :] = jnp.zeros((total - sure, cat_width), f32)
    prob_part[sure:, :] = jnp.zeros((total - sure, lat_width), f32)

    def key_grads(u, source, target, rhs, first, last):
        is_upper, kt = places[u]
        part = dot_nn(source[...], rhs[half_of(is_upper), :row_count, first:last])
        if groups[u][0] <= tile_count // 2:
            target[tile_rows(kt, counts[u]), first:last] = part
        else:
            target[tile_rows(kt, counts[u]), first:last] += part

    def key_steps(u):
        widths = [(first, min(first + 256, cat_width)) for first in range(0, cat_width, 256)]
        steps = []
        for first, last in widths:
            steps.append(functools.partial(key_grads, u, ds_ref.at[tiles[u]], score_part, q_ref, first, last))
            if last <= lat_width:
                steps.append(functools.partial(key_grads, u, prob_scr.at[u % 2, : counts[u] * key_tile], prob_part, dl_ref, first, last))
        return steps

    pending = []
    for i, (u, chunk) in enumerate(work):
        d_prob = ahead
        if i + 1 < len(work):
            ahead = prob_dot(*work[i + 1])
        left = len(chunks) - i % len(chunks)
        for j in range(-(-len(pending) // left)):
            pending.pop(0)()
        is_upper, kt = places[u]
        delta = pick(is_upper, deltas[1], deltas[0])
        prob = e_scr[tiles[u], chunk] * factors[u][:, chunk]
        ds_ref[tiles[u], chunk] = (prob * (d_prob - delta[:, chunk])).astype(bf16)
        prob_scr[u % 2, : counts[u] * key_tile, chunk] = prob.astype(bf16)
        if left == 1:
            pending = key_steps(u)
    for key_step in pending:
        key_step()

    pack(1, head_count, span_ref, score_part, prob_part, send_ref)


def pack(side, head_count, span_ref, score_part, prob_part, out_ref):
    total, cat_width = score_part.shape
    lat_width = prob_part.shape[1]
    z_count = lax.axis_size("ctx") // 2
    piece_rows = total // z_count // 2 // head_count
    span = total // z_count // 4
    per_span = span // piece_rows
    on = piece_rows % 32 == 0
    size = z_count * folded(piece_rows, cat_width, on)[0]
    owner_core = lax.rem(lax.axis_index("ctx") + side, 2)
    for quarter in range(head_count):
        rows = []
        for other in range(z_count):
            block = span_ref[quarter // per_span, 2 * other + owner_core]
            start = block * span + quarter % per_span * piece_rows
            here = pl.ds(pl.multiple_of(start, piece_rows), piece_rows)
            terms = score_part[here, :] * (1.0 / log2_e)
            latent = terms[:, :lat_width] + prob_part[here, :]
            rows.append(fold(jnp.concatenate([latent, terms[:, lat_width:]], axis=1), on))
        out_ref[quarter * size : (quarter + 1) * size, :] = jnp.concatenate(rows, axis=0).astype(bf16)


def query_kernel(
    scale, span_ref, keys_ref, ds_ref, w_uk_ref, nope_ref, rope_ref, dq_scr
):
    tile_total, row_count = ds_ref.shape[0] // key_tile, ds_ref.shape[1]
    tile_count = tile_total - 1
    heads, nope_width, lat_width = w_uk_ref.shape
    span = row_count // heads
    cat_width = keys_ref.shape[1]
    my_lower = span_ref[0, lax.axis_index("ctx")]
    places = [tile_place(u, tile_count, span, my_lower) for u in range(tile_total)]
    sure = tile_count // 2 + 1
    dq_scr[1] = dot_tn(keys_ref[: sure * key_tile, :], ds_ref[: sure * key_tile, :])
    dq_scr[0] = dot_tn(keys_ref[:key_tile, :], ds_ref[tile_count * key_tile :, :])
    for u, (is_upper, kt) in enumerate(places):
        if not isinstance(is_upper, bool):
            dq_scr[half_of(is_upper)] += dot_tn(keys_ref[tile_rows(kt), :], ds_ref[tile_rows(u), :])
    for pair in range(heads // 2):
        wide = slice(pair * 2 * span, (pair + 1) * 2 * span)
        turned = [jnp.transpose(dq_scr[s, :, wide]) * scale for s in range(2)]
        for p in range(2):
            head = 2 * pair + p
            rows = jnp.concatenate([t[p * span : (p + 1) * span, :lat_width] for t in turned], axis=0)
            nope_ref[:, head * nope_width : (head + 1) * nope_width] = dot_nt(
                rows.astype(bf16), w_uk_ref[head]
            ).astype(bf16)
        rope = [
            jnp.concatenate([t[p * span : (p + 1) * span, lat_width:] for t in turned], axis=0) for p in range(2)
        ]
        width = 2 * (cat_width - lat_width)
        rope_ref[:, pair * width : (pair + 1) * width] = jnp.concatenate(rope, axis=1).astype(bf16)


def pair_sum_kernel(keep_ref, recv_ref, own_ref, *send_refs):
    head = lax.axis_index("head")
    share = own_ref.shape[0]

    def both(target):
        rows = pl.ds(pl.multiple_of(target * share, share), share)
        return keep_ref[rows, :].astype(f32) + recv_ref[rows, :].astype(f32)

    own_ref[...] = both(head)
    for m, ref in zip(range(len(send_refs), 0, -1), send_refs):
        ref[...] = both(head ^ m).astype(bf16)


def head_sum_kernel(*refs):
    z_count = refs[0].shape[0] // refs[-2].shape[0]
    head_count = len(refs) - 1 - z_count
    terms, own_ref, send_refs, total = refs[:head_count], refs[head_count], refs[head_count + 1 : -1], refs[-1]
    total[...] = functools.reduce(jnp.add, [ref[...].astype(f32) for ref in terms])
    rows = own_ref.shape[0]
    z = lax.axis_index("ctx") // 2

    def share(k):
        return total[pl.ds(pl.multiple_of((z ^ k) * rows, rows), rows), :]

    own_ref[...] = share(0)
    for k, ref in zip(range(len(send_refs), 0, -1), send_refs):
        ref[...] = share(k).astype(bf16)


def chip_sum_kernel(*refs):
    refs[-1][...] = functools.reduce(jnp.add, [ref[...].astype(f32) for ref in refs[:-1]]).astype(bf16)


def norm_back_kernel(cache_t_ref, gain_ref, *refs):
    shares, (out_hbm, total, out_ref, sems) = refs[:-4], refs[-4:]
    head = lax.axis_index("head")
    rows = total.shape[0] // len(shares)
    lat_width = gain_ref.shape[0]
    for m, ref in enumerate(shares):
        total[pl.ds(pl.multiple_of((head ^ m) * rows, rows), rows), :] = unfold(
            ref[...].astype(f32), total.shape[1], rows % 32 == 0
        )
    blocks = [slice(j, min(j + 128, total.shape[1])) for j in range(0, total.shape[1], 128)]
    copies = [pltpu.make_async_copy(out_ref.at[b], out_hbm.at[b], sems.at[j]) for j, b in enumerate(blocks)]
    values = cache_t_ref[:lat_width, :].astype(f32)
    inverse = lax.rsqrt(jnp.mean(values * values, axis=0, keepdims=True) + eps_norm)
    out_ref[lat_width:, :] = jnp.transpose(total[:, lat_width:])
    copies[-1].start()
    scaled = jnp.transpose(total[:, :lat_width] * gain_ref[...].astype(f32)[None, :])
    inner = jnp.mean(values * scaled, axis=0, keepdims=True)
    factor = inverse * inverse * inverse * inner
    for block, copy in zip(blocks[:-1], copies):
        out_ref[block, :] = inverse * scaled[block] - values[block] * factor
        copy.start()
    for copy in copies:
        copy.wait()


def local(q_nope, q_rope, kv_cache, kv_gain, w_uk, w_uv, attn_out, d_out, span_table):
    shape = jax.ShapeDtypeStruct
    tok_rows, cat_width = kv_cache.shape
    heads, nope_width, lat_width = w_uk.shape
    value_width = w_uv.shape[2]
    rope_width = q_rope.shape[1] // heads
    span = tok_rows // 2
    row_count = span * heads
    scale = float(nope_width + rope_width) ** (-0.5)
    ctx_count, head_count = lax.axis_size("ctx"), lax.axis_size("head")
    z_count = ctx_count // 2
    total = ctx_count * tok_rows
    tile_total = total // key_tile + 1
    piece_rows = tok_rows // head_count
    cache_t = kv_cache.T
    spans = span_table.T

    def to_core(rows):
        return lax.ppermute(rows, "ctx", [(i, i ^ 1) for i in range(ctx_count)])

    def to_chip(rows, k):
        return lax.ppermute(rows, "ctx", [(i, i ^ (2 * k)) for i in range(ctx_count)])

    def to_head(rows, m):
        return lax.ppermute(rows, "head", [(j, j ^ m) for j in range(head_count)])

    on = piece_rows % 32 == 0
    piece = pl.pallas_call(
        piece_kernel,
        out_shape=shape(folded(piece_rows, cat_width, on), bf16),
        in_specs=[in_any],
        out_specs=in_vmem,
        scratch_shapes=[
            pltpu.VMEM((cat_width, tok_rows), bf16),
            pltpu.VMEM((tok_rows, cat_width), f32),
            pltpu.SemaphoreType.DMA,
        ],
        compiler_params=params(piece_mib),
        name="piece",
    )(cache_t)
    pieces = [to_chip(piece, k) for k in range(1, z_count)]
    keys_own = pl.pallas_call(
        functools.partial(own_kernel, on),
        out_shape=shape(folded(tok_rows, cat_width, on), bf16),
        in_specs=[in_vmem] * 2,
        out_specs=in_vmem,
        compiler_params=params(8),
        cost_estimate=pl.CostEstimate(flops=window_flops, bytes_accessed=mib, transcendentals=0),
        name="own_keys",
    )(cache_t, kv_gain)
    *pieces, keys_own = lax.optimization_barrier((*pieces, keys_own))
    pieces = pl.pallas_call(
        functools.partial(join_chips_kernel, on, cat_width),
        out_shape=shape(((z_count - 1) * piece.shape[0], piece.shape[1]), bf16),
        in_specs=[in_vmem] * z_count,
        out_specs=in_vmem,
        compiler_params=params(8),
        name="join_chips",
    )(kv_gain, *pieces)

    def join(rows, name):
        return pl.pallas_call(
            join_kernel,
            out_shape=shape((sum(r.shape[0] for r in rows), rows[0].shape[1]), bf16),
            in_specs=[in_vmem] * len(rows),
            out_specs=in_vmem,
            compiler_params=params(4),
            name=name,
        )(*rows)

    queries, d_latent = pl.pallas_call(
        functools.partial(project_kernel, scale * log2_e),
        out_shape=(shape((2, row_count, cat_width), bf16), shape((2, row_count + delta_rows, lat_width), bf16)),
        in_specs=[in_vmem] * 6 + [in_any],
        out_specs=(in_vmem,) * 2,
        scratch_shapes=[pltpu.VMEM((heads // 2, 2, 8, 2 * span), f32)],
        compiler_params=params(project_mib),
        cost_estimate=pl.CostEstimate(
            flops=8 * row_count * nope_width * lat_width, bytes_accessed=12 * mib, transcendentals=0
        ),
        name="project",
    )(q_nope, q_rope, w_uk, d_out, attn_out, w_uv, pieces)
    pieces = [pieces] + [to_head(pieces, m) for m in range(1, head_count)]
    *pieces, queries, d_latent = lax.optimization_barrier((*pieces, queries, d_latent))
    pieces = join([keys_own] + pieces, "join_heads")
    sib_pieces = to_core(pieces)
    aligned = piece_rows % 16 == 0
    placed = pl.pallas_call(
        functools.partial(place_rows, head_count, 0),
        out_shape=shape((total, cat_width), bf16 if aligned else f32),
        in_specs=[in_smem, in_vmem],
        out_specs=in_vmem,
        compiler_params=params(8),
        name="place",
    )(spans, pieces)
    sib_pieces, placed = lax.optimization_barrier((sib_pieces, placed))

    piece_shape = piece.shape
    share_shape = (z_count * piece_shape[0], piece_shape[1])
    all_shape = (head_count * share_shape[0], piece_shape[1])
    keys, d_score, send, score_part, prob_part = pl.pallas_call(
        functools.partial(attend_kernel, head_count),
        out_shape=(
            shape((total, cat_width), bf16),
            shape((tile_total * key_tile, row_count), bf16),
            shape(all_shape, bf16),
            shape((total, cat_width), f32),
            shape((total, lat_width), f32),
        ),
        in_specs=[in_smem] + [in_vmem] * 4,
        input_output_aliases={2: 0} if aligned else {},
        out_specs=(in_vmem,) * 5,
        scratch_shapes=[
            pltpu.VMEM((tile_total * key_tile, row_count), f32),
            pltpu.VMEM((2, key_tile, row_count), bf16),
        ],
        compiler_params=params(attend_mib if total <= 2048 else 56),
        cost_estimate=pl.CostEstimate(
            flops=2 * tile_total * key_tile * row_count * (2 * cat_width + 2 * lat_width),
            bytes_accessed=12 * mib,
            transcendentals=tile_total * key_tile * row_count,
        ),
        name="attend",
    )(spans, sib_pieces, placed, queries, d_latent)

    recv = to_core(send)
    keep = pl.pallas_call(
        functools.partial(pack, 0, head_count),
        out_shape=shape(all_shape, bf16),
        in_specs=[in_smem] + [in_vmem] * 2,
        out_specs=in_vmem,
        compiler_params=params(6),
        name="pack_keep",
    )(spans, score_part, prob_part)
    sums = pl.pallas_call(
        pair_sum_kernel,
        out_shape=(shape(share_shape, f32),) + (shape(share_shape, bf16),) * (head_count - 1),
        in_specs=[in_vmem] * 2,
        out_specs=(in_vmem,) * head_count,
        compiler_params=params(4),
        name="pair_sum",
    )(keep, recv)
    *sums, d_score = lax.optimization_barrier((*sums, d_score))
    d_q_nope, d_q_rope = pl.pallas_call(
        functools.partial(query_kernel, scale),
        out_shape=(shape(q_nope.shape, bf16), shape(q_rope.shape, bf16)),
        in_specs=[in_smem] + [in_vmem] * 3,
        out_specs=(in_vmem,) * 2,
        scratch_shapes=[pltpu.VMEM((2, cat_width, row_count), f32)],
        compiler_params=params(query_mib),
        cost_estimate=pl.CostEstimate(
            flops=2 * tile_total * key_tile * row_count * cat_width,
            bytes_accessed=8 * mib,
            transcendentals=0,
        ),
        name="query_grads",
    )(spans, keys, d_score, w_uk)
    terms = [sums[0]] + [to_head(rows, m) for m, rows in zip(range(head_count - 1, 0, -1), sums[1:])]
    *terms, d_q_nope, d_q_rope = lax.optimization_barrier((*terms, d_q_nope, d_q_rope))
    sums = pl.pallas_call(
        head_sum_kernel,
        out_shape=(shape(piece_shape, f32),) + (shape(piece_shape, bf16),) * (z_count - 1),
        in_specs=[in_vmem] * head_count,
        out_specs=(in_vmem,) * z_count,
        scratch_shapes=[pltpu.VMEM(share_shape, f32)],
        compiler_params=params(4),
        name="head_sum",
    )(*terms)
    terms = [sums[0]] + [to_chip(rows, k) for k, rows in zip(range(z_count - 1, 0, -1), sums[1:])]
    share = pl.pallas_call(
        chip_sum_kernel,
        out_shape=shape(piece_shape, bf16),
        in_specs=[in_vmem] * z_count,
        out_specs=in_vmem,
        compiler_params=params(4),
        name="chip_sum",
    )(*terms)
    shares = [share] + [to_head(share, m) for m in range(1, head_count)]
    d_cache_t = pl.pallas_call(
        norm_back_kernel,
        out_shape=shape((cat_width, tok_rows), f32),
        in_specs=[in_vmem] * (2 + head_count),
        out_specs=in_any,
        scratch_shapes=[
            pltpu.VMEM((tok_rows, cat_width), f32),
            pltpu.VMEM((cat_width, tok_rows), f32),
            pltpu.SemaphoreType.DMA((-(-cat_width // 128),)),
        ],
        compiler_params=params(8),
        name="norm_back",
    )(cache_t, kv_gain, *shares)
    return (d_q_nope, d_q_rope, d_cache_t.T)


def solution(mesh):
    in_specs = (
        P("ctx", "head"),
        P("ctx", "head"),
        P("ctx", None),
        P(),
        P("head", None, None),
        P("head", None, None),
        P("ctx", "head"),
        P("ctx", "head"),
        P(),
    )
    out_specs = (P("ctx", "head"), P("ctx", "head"), P("ctx", None))
    return jax.shard_map(local, mesh=mesh, in_specs=in_specs, out_specs=out_specs, check_vma=False)
```

```python
import functools

import jax
import jax.numpy as jnp
from jax import lax
from jax.experimental import pallas as pl
from jax.experimental.pallas import tpu as pltpu
from jax.sharding import PartitionSpec as P

neg_big = -1e30
eps_norm = 1e-06
log2_e = 1.4426950408889634
key_tile = 256
mib = 1024 * 1024
piece_mib = 53.8
query_mib = 16
attend_mib = 28
project_mib = 12
window_flops = 8 * 10**9
delta_rows = 16
row_chunk = 512
f32 = jnp.float32
bf16 = jnp.bfloat16
in_vmem = pl.BlockSpec(memory_space=pltpu.VMEM)
in_hbm = pl.BlockSpec(memory_space=pltpu.HBM)
in_any = pl.BlockSpec(memory_space=pl.ANY)
in_smem = pl.BlockSpec(memory_space=pltpu.SMEM)


def dot_nn(left, right):
    return lax.dot_general(left, right, (((1,), (0,)), ((), ())), preferred_element_type=f32)


def dot_nt(left, right):
    return lax.dot_general(left, right, (((1,), (1,)), ((), ())), preferred_element_type=f32)


def dot_tn(left, right):
    return lax.dot_general(left, right, (((0,), (0,)), ((), ())), preferred_element_type=f32)


def fold(block, on):
    if not on:
        return block
    rows, width = block.shape
    whole = width // 128
    half = rows // 2
    last = jnp.concatenate([block[:half, whole * 128 :], block[half:, whole * 128 :]], axis=1)
    return jnp.concatenate([block[:, j * 128 : (j + 1) * 128] for j in range(whole)] + [last], axis=0)


def unfold(block, width, on):
    if not on:
        return block
    rows = block.shape[0] * 128 // width
    whole = width // 128
    last = block[whole * rows :]
    edge = jnp.concatenate([last[:, : width - whole * 128], last[:, width - whole * 128 :]], axis=0)
    return jnp.concatenate([block[j * rows : (j + 1) * rows] for j in range(whole)] + [edge], axis=1)


def folded(rows, width, on):
    return (rows * width // 128, 128) if on else (rows, width)


def params(size):
    return pltpu.CompilerParams(vmem_limit_bytes=int(size * mib))


def piece_kernel(cache_t_hbm, piece_ref, cache_scr, rows_scr, sem):
    copy = pltpu.make_async_copy(cache_t_hbm, cache_scr, sem)
    copy.start()
    copy.wait()
    rows_scr[...] = jnp.transpose(cache_scr[...].astype(f32))
    rows = rows_scr.shape[0] // lax.axis_size("head")
    start = pl.multiple_of(lax.axis_index("head") * rows, rows)
    piece_ref[...] = fold(rows_scr[pl.ds(start, rows), :], rows % 32 == 0).astype(bf16)


def normalised(rows, gain):
    width = gain.shape[1]
    latent = rows[:, :width]
    inverse = lax.rsqrt(jnp.mean(latent * latent, axis=1, keepdims=True) + eps_norm)
    return jnp.concatenate([latent * inverse * gain, rows[:, width:]], axis=1)


def own_kernel(on, cache_t_ref, gain_ref, out_ref):
    rows = jnp.transpose(cache_t_ref[...].astype(f32))
    out_ref[...] = fold(normalised(rows, gain_ref[...].astype(f32)[None, :]), on).astype(bf16)


def join_chips_kernel(on, width, gain_ref, *refs):
    gain = gain_ref[...].astype(f32)[None, :]
    rows = jnp.concatenate([unfold(ref[...].astype(f32), width, on) for ref in refs[:-1]], axis=0)
    rows = normalised(rows, gain)
    size = rows.shape[0] // (len(refs) - 1)
    parts = [fold(rows[i * size : (i + 1) * size], on) for i in range(len(refs) - 1)]
    refs[-1][...] = jnp.concatenate(parts, axis=0).astype(bf16)


def project_kernel(
    factor, nope_ref, rope_ref, w_uk_ref, grad_ref, out_ref, w_uv_ref, unused_ref, q_ref, dl_ref, delta_scr
):
    heads, lat_width, value_width = w_uv_ref.shape
    nope_width = w_uk_ref.shape[1]
    span = grad_ref.shape[0] // 2
    rope_width = rope_ref.shape[1] // heads
    row_count = heads * span
    pairs = heads // 2
    ones = jnp.ones((8, value_width), bf16)
    for i in range(pairs):
        rope = (rope_ref[:, 2 * i * rope_width : 2 * (i + 1) * rope_width].astype(f32) * factor).astype(bf16)
        wide = slice(2 * i * value_width, 2 * (i + 1) * value_width)
        products = grad_ref[:, wide].astype(f32) * out_ref[:, wide].astype(f32)
        for p in range(2):
            head = 2 * i + p
            rows = slice(head * span, (head + 1) * span)
            q_lat = dot_nn(nope_ref[:, head * nope_width : (head + 1) * nope_width], w_uk_ref[head])
            q_lat = (q_lat * factor).astype(bf16)
            d_lat = dot_nt(grad_ref[:, head * value_width : (head + 1) * value_width], w_uv_ref[head]).astype(bf16)
            for s in range(2):
                tokens = slice(s * span, (s + 1) * span)
                q_ref[s, rows, :lat_width] = q_lat[tokens]
                q_ref[s, rows, lat_width:] = rope[tokens, p * rope_width : (p + 1) * rope_width]
                dl_ref[s, rows, :] = d_lat[tokens]
        for s in range(2):
            tokens = slice(s * span, (s + 1) * span)
            product = jnp.concatenate([products[tokens, :value_width], products[tokens, value_width:]], axis=0)
            high = product.astype(bf16)
            low = (product - high.astype(f32)).astype(bf16)
            delta_scr[i, s] = dot_nt(ones, high) + dot_nt(ones, low)

    per_row = min(lat_width // (2 * span), pairs)
    for s in range(2):
        rows = []
        for start in range(0, pairs, per_row):
            rows.append(jnp.concatenate([delta_scr[i, s, :1] for i in range(start, start + per_row)], axis=1))
        width = rows[0].shape[1]
        full = jnp.concatenate(rows + [jnp.zeros((8 - len(rows), width), f32)], axis=0)
        high = full.astype(bf16).astype(f32)
        both = jnp.concatenate([high, full - high], axis=0)
        if width < lat_width:
            both = jnp.concatenate([both, jnp.zeros((delta_rows, lat_width - width), f32)], axis=1)
        dl_ref[s, row_count:, :] = both.astype(bf16)


def join_kernel(*refs):
    if any(ref.shape[0] % 16 for ref in refs):
        refs[-1][...] = jnp.concatenate([ref[...].astype(f32) for ref in refs[:-1]], axis=0).astype(bf16)
        return
    start = 0
    for ref in refs[:-1]:
        size = ref.shape[0]
        refs[-1][start : start + size, :] = ref[...]
        start += size


def tile_groups(tile_count):
    return [(u, u + 1) for u in range(tile_count + 1)]


def tile_place(u, tile_count, span, lower_block):
    per_tile = key_tile // span
    upper_count = (tile_count * per_tile - 1 - lower_block) // per_tile + 1
    if u <= tile_count // 2:
        return True, u
    if u == tile_count:
        return False, 0
    is_upper = u < upper_count
    return is_upper, jnp.where(is_upper, u, tile_count - u)


def pick(is_upper, upper, lower):
    if isinstance(is_upper, bool):
        return upper if is_upper else lower
    return jnp.where(is_upper, upper, lower)


def half_of(is_upper):
    return int(is_upper) if isinstance(is_upper, bool) else is_upper.astype(jnp.int32)


def tile_rows(kt, count=1):
    if isinstance(kt, int):
        return slice(kt * key_tile, (kt + count) * key_tile)
    return pl.ds(pl.multiple_of(kt * key_tile, key_tile), key_tile)


def place_rows(head_count, side, span_ref, source, keys_ref):
    total, cat_width = keys_ref.shape
    z_count = lax.axis_size("ctx") // 2
    span = total // z_count // 4
    piece_rows = 2 * span // head_count
    per_span = span // piece_rows
    on = piece_rows % 32 == 0
    start = folded(2 * span, cat_width, on)[0]
    size = folded(piece_rows, cat_width, on)[0]
    me, head = lax.axis_index("ctx"), lax.axis_index("head")
    source = source if piece_rows % 16 == 0 else source[...].astype(f32)
    rows = unfold(source[:start, :], cat_width, on).astype(keys_ref.dtype)
    for s in range(2):
        row = pl.multiple_of(span_ref[s, me ^ side] * span, span)
        keys_ref[pl.ds(row, span), :] = rows[s * span : (s + 1) * span, :]
    for m in range(head_count):
        quarter = head ^ m
        for k in range(1, z_count):
            owner = 2 * (me // 2 ^ k) + lax.rem(me + side, 2)
            row = span_ref[quarter // per_span, owner] * span + lax.rem(quarter, per_span) * piece_rows
            rows = unfold(source[start : start + size, :], cat_width, on)
            keys_ref[pl.ds(pl.multiple_of(row, piece_rows), piece_rows), :] = rows.astype(keys_ref.dtype)
            start += size


def attend_kernel(head_count, *refs):
    span_ref, sib_pieces, placed_ref, q_ref, dl_ref = refs[:5]
    keys_ref, ds_ref, send_ref, score_part, prob_part, e_scr, prob_scr = refs[5:]
    half_count, row_count, cat_width = q_ref.shape
    lat_width = dl_ref.shape[2]
    total = keys_ref.shape[0]
    tile_count = total // key_tile
    span = total // lax.axis_size("ctx") // 2
    me = lax.axis_index("ctx")
    if placed_ref.dtype == keys_ref.dtype:
        place_rows(head_count, 1, span_ref, sib_pieces, keys_ref)
    else:
        place_rows(head_count, 1, span_ref, sib_pieces, placed_ref)
        keys_ref[...] = placed_ref[...].astype(bf16)

    my_lower, my_upper = span_ref[0, me], span_ref[1, me]
    chunks = [slice(n, n + min(row_chunk, row_count)) for n in range(0, row_count, row_chunk)]
    groups = tile_groups(tile_count)
    counts = [last - first for first, last in groups]
    tiles = [slice(first * key_tile, last * key_tile) for first, last in groups]
    places = [tile_place(first, tile_count, span, my_lower) for first, last in groups]
    work = [(g, chunk) for g in range(len(groups)) for chunk in chunks]
    step_shape = (key_tile, min(row_chunk, row_count))
    key_step = lax.broadcasted_iota(jnp.int32, step_shape, 0)
    row_step = lax.rem(lax.broadcasted_iota(jnp.int32, step_shape, 1), span)
    step = row_step - key_step

    def score_dot(u, chunk):
        is_upper, kt = places[u]
        return dot_nt(keys_ref[tile_rows(kt, counts[u]), :], q_ref[half_of(is_upper), chunk])

    top_parts, sum_parts = {}, {}
    ahead = score_dot(*work[0])
    for i, (u, chunk) in enumerate(work):
        scores = ahead
        if i + 1 < len(work):
            ahead = score_dot(*work[i + 1])
        is_upper, kt = places[u]
        if groups[u][0] >= tile_count // 2:
            base = kt * key_tile - pick(is_upper, my_upper, my_lower) * span
            scores = jnp.where(step >= base, scores, neg_big)
        top = jnp.max(scores, axis=0, keepdims=True)
        weights = jnp.exp2(scores - top)
        e_scr[tiles[u], chunk] = weights
        top_parts.setdefault(u, []).append(top)
        sum_parts.setdefault(u, []).append(jnp.sum(weights, axis=0, keepdims=True))
    tops = [jnp.concatenate(top_parts[u], axis=1) for u in range(len(groups))]
    sums = [jnp.concatenate(sum_parts[u], axis=1) for u in range(len(groups))]

    def prob_dot(u, chunk):
        is_upper, kt = places[u]
        return dot_nt(keys_ref[tile_rows(kt, counts[u]), :lat_width], dl_ref[half_of(is_upper), chunk])

    ahead = prob_dot(*work[0])
    row_top, row_sum = [], []
    for s in range(2):
        kept = [jnp.where(half_of(is_upper) == s, top, neg_big) for (is_upper, kt), top in zip(places, tops)]
        best = functools.reduce(jnp.maximum, kept)
        row_top.append(best)
        row_sum.append(functools.reduce(jnp.add, [jnp.exp2(top - best) * add for top, add in zip(kept, sums)]))
    inverse = [1.0 / part for part in row_sum]
    factors = []
    for (is_upper, kt), top in zip(places, tops):
        best = pick(is_upper, row_top[1], row_top[0])
        factors.append(jnp.exp2(top - best) * pick(is_upper, inverse[1], inverse[0]))
    deltas = []
    for s in range(2):
        parts = dl_ref[s, row_count:, :].astype(f32)
        width = min(lat_width, row_count)
        rows = [parts[j : j + 1, :width] + parts[8 + j : 9 + j, :width] for j in range(row_count // width)]
        deltas.append(jnp.concatenate(rows, axis=1))
    sure = (tile_count // 2 + 1) * key_tile
    score_part[sure:, :] = jnp.zeros((total - sure, cat_width), f32)
    prob_part[sure:, :] = jnp.zeros((total - sure, lat_width), f32)

    def key_grads(u, source, target, rhs, first, last):
        is_upper, kt = places[u]
        part = dot_nn(source[...], rhs[half_of(is_upper), :row_count, first:last])
        if groups[u][0] <= tile_count // 2:
            target[tile_rows(kt, counts[u]), first:last] = part
        else:
            target[tile_rows(kt, counts[u]), first:last] += part

    def key_steps(u):
        widths = [(first, min(first + 256, cat_width)) for first in range(0, cat_width, 256)]
        steps = []
        for first, last in widths:
            steps.append(functools.partial(key_grads, u, ds_ref.at[tiles[u]], score_part, q_ref, first, last))
            if last <= lat_width:
                steps.append(functools.partial(key_grads, u, prob_scr.at[u % 2, : counts[u] * key_tile], prob_part, dl_ref, first, last))
        return steps

    pending = []
    for i, (u, chunk) in enumerate(work):
        d_prob = ahead
        if i + 1 < len(work):
            ahead = prob_dot(*work[i + 1])
        left = len(chunks) - i % len(chunks)
        for j in range(-(-len(pending) // left)):
            pending.pop(0)()
        is_upper, kt = places[u]
        delta = pick(is_upper, deltas[1], deltas[0])
        prob = e_scr[tiles[u], chunk] * factors[u][:, chunk]
        ds_ref[tiles[u], chunk] = (prob * (d_prob - delta[:, chunk])).astype(bf16)
        prob_scr[u % 2, : counts[u] * key_tile, chunk] = prob.astype(bf16)
        if left == 1:
            pending = key_steps(u)
    for key_step in pending:
        key_step()

    pack(1, head_count, span_ref, score_part, prob_part, send_ref)


def pack(side, head_count, span_ref, score_part, prob_part, out_ref):
    total, cat_width = score_part.shape
    lat_width = prob_part.shape[1]
    z_count = lax.axis_size("ctx") // 2
    piece_rows = total // z_count // 2 // head_count
    span = total // z_count // 4
    per_span = span // piece_rows
    on = piece_rows % 32 == 0
    size = z_count * folded(piece_rows, cat_width, on)[0]
    owner_core = lax.rem(lax.axis_index("ctx") + side, 2)
    for quarter in range(head_count):
        rows = []
        for other in range(z_count):
            block = span_ref[quarter // per_span, 2 * other + owner_core]
            start = block * span + quarter % per_span * piece_rows
            here = pl.ds(pl.multiple_of(start, piece_rows), piece_rows)
            terms = score_part[here, :] * (1.0 / log2_e)
            latent = terms[:, :lat_width] + prob_part[here, :]
            rows.append(fold(jnp.concatenate([latent, terms[:, lat_width:]], axis=1), on))
        out_ref[quarter * size : (quarter + 1) * size, :] = jnp.concatenate(rows, axis=0).astype(bf16)


def query_kernel(
    scale, span_ref, keys_ref, ds_ref, w_uk_ref, nope_ref, rope_ref, dq_scr
):
    tile_total, row_count = ds_ref.shape[0] // key_tile, ds_ref.shape[1]
    tile_count = tile_total - 1
    heads, nope_width, lat_width = w_uk_ref.shape
    span = row_count // heads
    cat_width = keys_ref.shape[1]
    my_lower = span_ref[0, lax.axis_index("ctx")]
    places = [tile_place(u, tile_count, span, my_lower) for u in range(tile_total)]
    sure = tile_count // 2 + 1
    dq_scr[1] = dot_tn(keys_ref[: sure * key_tile, :], ds_ref[: sure * key_tile, :])
    dq_scr[0] = dot_tn(keys_ref[:key_tile, :], ds_ref[tile_count * key_tile :, :])
    for u, (is_upper, kt) in enumerate(places):
        if not isinstance(is_upper, bool):
            dq_scr[half_of(is_upper)] += dot_tn(keys_ref[tile_rows(kt), :], ds_ref[tile_rows(u), :])
    for pair in range(heads // 2):
        wide = slice(pair * 2 * span, (pair + 1) * 2 * span)
        turned = [jnp.transpose(dq_scr[s, :, wide]) * scale for s in range(2)]
        for p in range(2):
            head = 2 * pair + p
            rows = jnp.concatenate([t[p * span : (p + 1) * span, :lat_width] for t in turned], axis=0)
            nope_ref[:, head * nope_width : (head + 1) * nope_width] = dot_nt(
                rows.astype(bf16), w_uk_ref[head]
            ).astype(bf16)
        rope = [
            jnp.concatenate([t[p * span : (p + 1) * span, lat_width:] for t in turned], axis=0) for p in range(2)
        ]
        width = 2 * (cat_width - lat_width)
        rope_ref[:, pair * width : (pair + 1) * width] = jnp.concatenate(rope, axis=1).astype(bf16)


def pair_sum_kernel(keep_ref, recv_ref, own_ref, *send_refs):
    head = lax.axis_index("head")
    share = own_ref.shape[0]

    def both(target):
        rows = pl.ds(pl.multiple_of(target * share, share), share)
        return keep_ref[rows, :].astype(f32) + recv_ref[rows, :].astype(f32)

    own_ref[...] = both(head)
    for m, ref in zip(range(len(send_refs), 0, -1), send_refs):
        ref[...] = both(head ^ m).astype(bf16)


def head_sum_kernel(*refs):
    z_count = refs[0].shape[0] // refs[-2].shape[0]
    head_count = len(refs) - 1 - z_count
    terms, own_ref, send_refs, total = refs[:head_count], refs[head_count], refs[head_count + 1 : -1], refs[-1]
    total[...] = functools.reduce(jnp.add, [ref[...].astype(f32) for ref in terms])
    rows = own_ref.shape[0]
    z = lax.axis_index("ctx") // 2

    def share(k):
        return total[pl.ds(pl.multiple_of((z ^ k) * rows, rows), rows), :]

    own_ref[...] = share(0)
    for k, ref in zip(range(len(send_refs), 0, -1), send_refs):
        ref[...] = share(k).astype(bf16)


def chip_sum_kernel(*refs):
    refs[-1][...] = functools.reduce(jnp.add, [ref[...].astype(f32) for ref in refs[:-1]]).astype(bf16)


def norm_back_kernel(cache_t_ref, gain_ref, *refs):
    shares, (out_hbm, total, out_ref, sems) = refs[:-4], refs[-4:]
    head = lax.axis_index("head")
    rows = total.shape[0] // len(shares)
    lat_width = gain_ref.shape[0]
    for m, ref in enumerate(shares):
        total[pl.ds(pl.multiple_of((head ^ m) * rows, rows), rows), :] = unfold(
            ref[...].astype(f32), total.shape[1], rows % 32 == 0
        )
    blocks = [slice(j, min(j + 128, total.shape[1])) for j in range(0, total.shape[1], 128)]
    copies = [pltpu.make_async_copy(out_ref.at[b], out_hbm.at[b], sems.at[j]) for j, b in enumerate(blocks)]
    values = cache_t_ref[:lat_width, :].astype(f32)
    inverse = lax.rsqrt(jnp.mean(values * values, axis=0, keepdims=True) + eps_norm)
    out_ref[lat_width:, :] = jnp.transpose(total[:, lat_width:])
    copies[-1].start()
    scaled = jnp.transpose(total[:, :lat_width] * gain_ref[...].astype(f32)[None, :])
    inner = jnp.mean(values * scaled, axis=0, keepdims=True)
    factor = inverse * inverse * inverse * inner
    for block, copy in zip(blocks[:-1], copies):
        out_ref[block, :] = inverse * scaled[block] - values[block] * factor
        copy.start()
    for copy in copies:
        copy.wait()


def local(q_nope, q_rope, kv_cache, kv_gain, w_uk, w_uv, attn_out, d_out, span_table):
    shape = jax.ShapeDtypeStruct
    tok_rows, cat_width = kv_cache.shape
    heads, nope_width, lat_width = w_uk.shape
    value_width = w_uv.shape[2]
    rope_width = q_rope.shape[1] // heads
    span = tok_rows // 2
    row_count = span * heads
    scale = float(nope_width + rope_width) ** (-0.5)
    ctx_count, head_count = lax.axis_size("ctx"), lax.axis_size("head")
    z_count = ctx_count // 2
    total = ctx_count * tok_rows
    tile_total = total // key_tile + 1
    piece_rows = tok_rows // head_count
    cache_t = kv_cache.T
    spans = span_table.T

    def to_core(rows):
        return lax.ppermute(rows, "ctx", [(i, i ^ 1) for i in range(ctx_count)])

    def to_chip(rows, k):
        return lax.ppermute(rows, "ctx", [(i, i ^ (2 * k)) for i in range(ctx_count)])

    def to_head(rows, m):
        return lax.ppermute(rows, "head", [(j, j ^ m) for j in range(head_count)])

    on = piece_rows % 32 == 0
    piece = pl.pallas_call(
        piece_kernel,
        out_shape=shape(folded(piece_rows, cat_width, on), bf16),
        in_specs=[in_any],
        out_specs=in_vmem,
        scratch_shapes=[
            pltpu.VMEM((cat_width, tok_rows), bf16),
            pltpu.VMEM((tok_rows, cat_width), f32),
            pltpu.SemaphoreType.DMA,
        ],
        compiler_params=params(piece_mib),
        name="piece",
    )(cache_t)
    pieces = [to_chip(piece, k) for k in range(1, z_count)]
    keys_own = pl.pallas_call(
        functools.partial(own_kernel, on),
        out_shape=shape(folded(tok_rows, cat_width, on), bf16),
        in_specs=[in_vmem] * 2,
        out_specs=in_vmem,
        compiler_params=params(8),
        cost_estimate=pl.CostEstimate(flops=window_flops, bytes_accessed=mib, transcendentals=0),
        name="own_keys",
    )(cache_t, kv_gain)
    *pieces, keys_own = lax.optimization_barrier((*pieces, keys_own))
    pieces = pl.pallas_call(
        functools.partial(join_chips_kernel, on, cat_width),
        out_shape=shape(((z_count - 1) * piece.shape[0], piece.shape[1]), bf16),
        in_specs=[in_vmem] * z_count,
        out_specs=in_vmem,
        compiler_params=params(8),
        name="join_chips",
    )(kv_gain, *pieces)

    def join(rows, name):
        return pl.pallas_call(
            join_kernel,
            out_shape=shape((sum(r.shape[0] for r in rows), rows[0].shape[1]), bf16),
            in_specs=[in_vmem] * len(rows),
            out_specs=in_vmem,
            compiler_params=params(4),
            name=name,
        )(*rows)

    queries, d_latent = pl.pallas_call(
        functools.partial(project_kernel, scale * log2_e),
        out_shape=(shape((2, row_count, cat_width), bf16), shape((2, row_count + delta_rows, lat_width), bf16)),
        in_specs=[in_vmem] * 6 + [in_any],
        out_specs=(in_vmem,) * 2,
        scratch_shapes=[pltpu.VMEM((heads // 2, 2, 8, 2 * span), f32)],
        compiler_params=params(project_mib),
        cost_estimate=pl.CostEstimate(
            flops=8 * row_count * nope_width * lat_width, bytes_accessed=12 * mib, transcendentals=0
        ),
        name="project",
    )(q_nope, q_rope, w_uk, d_out, attn_out, w_uv, pieces)
    pieces = [pieces] + [to_head(pieces, m) for m in range(1, head_count)]
    *pieces, queries, d_latent = lax.optimization_barrier((*pieces, queries, d_latent))
    pieces = join([keys_own] + pieces, "join_heads")
    sib_pieces = to_core(pieces)
    aligned = piece_rows % 16 == 0
    placed = pl.pallas_call(
        functools.partial(place_rows, head_count, 0),
        out_shape=shape((total, cat_width), bf16 if aligned else f32),
        in_specs=[in_smem, in_vmem],
        out_specs=in_vmem,
        compiler_params=params(8),
        name="place",
    )(spans, pieces)
    sib_pieces, placed = lax.optimization_barrier((sib_pieces, placed))

    piece_shape = piece.shape
    share_shape = (z_count * piece_shape[0], piece_shape[1])
    all_shape = (head_count * share_shape[0], piece_shape[1])
    keys, d_score, send, score_part, prob_part = pl.pallas_call(
        functools.partial(attend_kernel, head_count),
        out_shape=(
            shape((total, cat_width), bf16),
            shape((tile_total * key_tile, row_count), bf16),
            shape(all_shape, bf16),
            shape((total, cat_width), f32),
            shape((total, lat_width), f32),
        ),
        in_specs=[in_smem] + [in_vmem] * 4,
        input_output_aliases={2: 0} if aligned else {},
        out_specs=(in_vmem,) * 5,
        scratch_shapes=[
            pltpu.VMEM((tile_total * key_tile, row_count), f32),
            pltpu.VMEM((2, key_tile, row_count), bf16),
        ],
        compiler_params=params(attend_mib if total <= 2048 else 56),
        cost_estimate=pl.CostEstimate(
            flops=2 * tile_total * key_tile * row_count * (2 * cat_width + 2 * lat_width),
            bytes_accessed=12 * mib,
            transcendentals=tile_total * key_tile * row_count,
        ),
        name="attend",
    )(spans, sib_pieces, placed, queries, d_latent)

    recv = to_core(send)
    keep = pl.pallas_call(
        functools.partial(pack, 0, head_count),
        out_shape=shape(all_shape, bf16),
        in_specs=[in_smem] + [in_vmem] * 2,
        out_specs=in_vmem,
        compiler_params=params(6),
        name="pack_keep",
    )(spans, score_part, prob_part)
    sums = pl.pallas_call(
        pair_sum_kernel,
        out_shape=(shape(share_shape, f32),) + (shape(share_shape, bf16),) * (head_count - 1),
        in_specs=[in_vmem] * 2,
        out_specs=(in_vmem,) * head_count,
        compiler_params=params(4),
        name="pair_sum",
    )(keep, recv)
    *sums, d_score = lax.optimization_barrier((*sums, d_score))
    d_q_nope, d_q_rope = pl.pallas_call(
        functools.partial(query_kernel, scale),
        out_shape=(shape(q_nope.shape, bf16), shape(q_rope.shape, bf16)),
        in_specs=[in_smem] + [in_vmem] * 3,
        out_specs=(in_vmem,) * 2,
        scratch_shapes=[pltpu.VMEM((2, cat_width, row_count), f32)],
        compiler_params=params(query_mib),
        cost_estimate=pl.CostEstimate(
            flops=2 * tile_total * key_tile * row_count * cat_width,
            bytes_accessed=8 * mib,
            transcendentals=0,
        ),
        name="query_grads",
    )(spans, keys, d_score, w_uk)
    terms = [sums[0]] + [to_head(rows, m) for m, rows in zip(range(head_count - 1, 0, -1), sums[1:])]
    *terms, d_q_nope, d_q_rope = lax.optimization_barrier((*terms, d_q_nope, d_q_rope))
    sums = pl.pallas_call(
        head_sum_kernel,
        out_shape=(shape(piece_shape, f32),) + (shape(piece_shape, bf16),) * (z_count - 1),
        in_specs=[in_vmem] * head_count,
        out_specs=(in_vmem,) * z_count,
        scratch_shapes=[pltpu.VMEM(share_shape, f32)],
        compiler_params=params(4),
        name="head_sum",
    )(*terms)
    terms = [sums[0]] + [to_chip(rows, k) for k, rows in zip(range(z_count - 1, 0, -1), sums[1:])]
    share = pl.pallas_call(
        chip_sum_kernel,
        out_shape=shape(piece_shape, bf16),
        in_specs=[in_vmem] * z_count,
        out_specs=in_vmem,
        compiler_params=params(4),
        name="chip_sum",
    )(*terms)
    shares = [share] + [to_head(share, m) for m in range(1, head_count)]
    d_cache_t = pl.pallas_call(
        norm_back_kernel,
        out_shape=shape((cat_width, tok_rows), f32),
        in_specs=[in_vmem] * (2 + head_count),
        out_specs=in_any,
        scratch_shapes=[
            pltpu.VMEM((tok_rows, cat_width), f32),
            pltpu.VMEM((cat_width, tok_rows), f32),
            pltpu.SemaphoreType.DMA((-(-cat_width // 128),)),
        ],
        compiler_params=params(8),
        name="norm_back",
    )(cache_t, kv_gain, *shares)
    return (d_q_nope, d_q_rope, d_cache_t.T)


def solution(mesh):
    in_specs = (
        P("ctx", "head"),
        P("ctx", "head"),
        P("ctx", None),
        P(),
        P("head", None, None),
        P("head", None, None),
        P("ctx", "head"),
        P("ctx", "head"),
        P(),
    )
    out_specs = (P("ctx", "head"), P("ctx", "head"), P("ctx", None))
    return jax.shard_map(local, mesh=mesh, in_specs=in_specs, out_specs=out_specs, check_vma=False)
```

```python
import functools

import jax
import jax.numpy as jnp
from jax import lax
from jax.experimental import pallas as pl
from jax.experimental.pallas import tpu as pltpu
from jax.sharding import PartitionSpec as P

neg_big = -1e30
eps_norm = 1e-06
log2_e = 1.4426950408889634
key_tile = 256
mib = 1024 * 1024
piece_mib = 53.8
query_mib = 16
attend_mib = 28
project_mib = 12
window_flops = 8 * 10**9
delta_rows = 16
row_chunk = 256
dots_ahead = 2
f32 = jnp.float32
bf16 = jnp.bfloat16
in_vmem = pl.BlockSpec(memory_space=pltpu.VMEM)
in_hbm = pl.BlockSpec(memory_space=pltpu.HBM)
in_any = pl.BlockSpec(memory_space=pl.ANY)
in_smem = pl.BlockSpec(memory_space=pltpu.SMEM)


def dot_nn(left, right):
    return lax.dot_general(left, right, (((1,), (0,)), ((), ())), preferred_element_type=f32)


def dot_nt(left, right):
    return lax.dot_general(left, right, (((1,), (1,)), ((), ())), preferred_element_type=f32)


def dot_tn(left, right):
    return lax.dot_general(left, right, (((0,), (0,)), ((), ())), preferred_element_type=f32)


def fold(block, on):
    if not on:
        return block
    rows, width = block.shape
    whole = width // 128
    half = rows // 2
    last = jnp.concatenate([block[:half, whole * 128 :], block[half:, whole * 128 :]], axis=1)
    return jnp.concatenate([block[:, j * 128 : (j + 1) * 128] for j in range(whole)] + [last], axis=0)


def unfold(block, width, on):
    if not on:
        return block
    rows = block.shape[0] * 128 // width
    whole = width // 128
    last = block[whole * rows :]
    edge = jnp.concatenate([last[:, : width - whole * 128], last[:, width - whole * 128 :]], axis=0)
    return jnp.concatenate([block[j * rows : (j + 1) * rows] for j in range(whole)] + [edge], axis=1)


def folded(rows, width, on):
    return (rows * width // 128, 128) if on else (rows, width)


def params(size):
    return pltpu.CompilerParams(vmem_limit_bytes=int(size * mib))


def piece_kernel(cache_t_hbm, piece_ref, cache_scr, rows_scr, sem):
    copy = pltpu.make_async_copy(cache_t_hbm, cache_scr, sem)
    copy.start()
    copy.wait()
    rows_scr[...] = jnp.transpose(cache_scr[...].astype(f32))
    rows = rows_scr.shape[0] // lax.axis_size("head")
    start = pl.multiple_of(lax.axis_index("head") * rows, rows)
    piece_ref[...] = fold(rows_scr[pl.ds(start, rows), :], rows % 32 == 0).astype(bf16)


def normalised(rows, gain):
    width = gain.shape[1]
    latent = rows[:, :width]
    inverse = lax.rsqrt(jnp.mean(latent * latent, axis=1, keepdims=True) + eps_norm)
    return jnp.concatenate([latent * inverse * gain, rows[:, width:]], axis=1)


def own_kernel(on, cache_t_ref, gain_ref, out_ref):
    rows = jnp.transpose(cache_t_ref[...].astype(f32))
    out_ref[...] = fold(normalised(rows, gain_ref[...].astype(f32)[None, :]), on).astype(bf16)


def join_chips_kernel(on, width, gain_ref, *refs):
    gain = gain_ref[...].astype(f32)[None, :]
    rows = jnp.concatenate([unfold(ref[...].astype(f32), width, on) for ref in refs[:-1]], axis=0)
    rows = normalised(rows, gain)
    size = rows.shape[0] // (len(refs) - 1)
    parts = [fold(rows[i * size : (i + 1) * size], on) for i in range(len(refs) - 1)]
    refs[-1][...] = jnp.concatenate(parts, axis=0).astype(bf16)


def project_kernel(
    factor, nope_ref, rope_ref, w_uk_ref, grad_ref, out_ref, w_uv_ref, unused_ref, q_ref, dl_ref, delta_scr
):
    heads, lat_width, value_width = w_uv_ref.shape
    nope_width = w_uk_ref.shape[1]
    span = grad_ref.shape[0] // 2
    rope_width = rope_ref.shape[1] // heads
    row_count = heads * span
    pairs = heads // 2
    ones = jnp.ones((8, value_width), bf16)
    for i in range(pairs):
        rope = (rope_ref[:, 2 * i * rope_width : 2 * (i + 1) * rope_width].astype(f32) * factor).astype(bf16)
        wide = slice(2 * i * value_width, 2 * (i + 1) * value_width)
        products = grad_ref[:, wide].astype(f32) * out_ref[:, wide].astype(f32)
        for p in range(2):
            head = 2 * i + p
            rows = slice(head * span, (head + 1) * span)
            q_lat = dot_nn(nope_ref[:, head * nope_width : (head + 1) * nope_width], w_uk_ref[head])
            q_lat = (q_lat * factor).astype(bf16)
            d_lat = dot_nt(grad_ref[:, head * value_width : (head + 1) * value_width], w_uv_ref[head]).astype(bf16)
            for s in range(2):
                tokens = slice(s * span, (s + 1) * span)
                q_ref[s, rows, :lat_width] = q_lat[tokens]
                q_ref[s, rows, lat_width:] = rope[tokens, p * rope_width : (p + 1) * rope_width]
                dl_ref[s, rows, :] = d_lat[tokens]
        for s in range(2):
            tokens = slice(s * span, (s + 1) * span)
            product = jnp.concatenate([products[tokens, :value_width], products[tokens, value_width:]], axis=0)
            high = product.astype(bf16)
            low = (product - high.astype(f32)).astype(bf16)
            delta_scr[i, s] = dot_nt(ones, high) + dot_nt(ones, low)

    per_row = min(lat_width // (2 * span), pairs)
    for s in range(2):
        rows = []
        for start in range(0, pairs, per_row):
            rows.append(jnp.concatenate([delta_scr[i, s, :1] for i in range(start, start + per_row)], axis=1))
        width = rows[0].shape[1]
        full = jnp.concatenate(rows + [jnp.zeros((8 - len(rows), width), f32)], axis=0)
        high = full.astype(bf16).astype(f32)
        both = jnp.concatenate([high, full - high], axis=0)
        if width < lat_width:
            both = jnp.concatenate([both, jnp.zeros((delta_rows, lat_width - width), f32)], axis=1)
        dl_ref[s, row_count:, :] = both.astype(bf16)


def join_kernel(*refs):
    if any(ref.shape[0] % 16 for ref in refs):
        refs[-1][...] = jnp.concatenate([ref[...].astype(f32) for ref in refs[:-1]], axis=0).astype(bf16)
        return
    start = 0
    for ref in refs[:-1]:
        size = ref.shape[0]
        refs[-1][start : start + size, :] = ref[...]
        start += size


def tile_groups(tile_count):
    return [(u, u + 1) for u in range(tile_count + 1)]


def tile_place(u, tile_count, span, lower_block):
    per_tile = key_tile // span
    upper_count = (tile_count * per_tile - 1 - lower_block) // per_tile + 1
    if u <= tile_count // 2:
        return True, u
    if u == tile_count:
        return False, 0
    is_upper = u < upper_count
    return is_upper, jnp.where(is_upper, u, tile_count - u)


def pick(is_upper, upper, lower):
    if isinstance(is_upper, bool):
        return upper if is_upper else lower
    return jnp.where(is_upper, upper, lower)


def half_of(is_upper):
    return int(is_upper) if isinstance(is_upper, bool) else is_upper.astype(jnp.int32)


def tile_rows(kt, count=1):
    if isinstance(kt, int):
        return slice(kt * key_tile, (kt + count) * key_tile)
    return pl.ds(pl.multiple_of(kt * key_tile, key_tile), key_tile)


def place_rows(head_count, side, span_ref, source, keys_ref):
    total, cat_width = keys_ref.shape
    z_count = lax.axis_size("ctx") // 2
    span = total // z_count // 4
    piece_rows = 2 * span // head_count
    per_span = span // piece_rows
    on = piece_rows % 32 == 0
    start = folded(2 * span, cat_width, on)[0]
    size = folded(piece_rows, cat_width, on)[0]
    me, head = lax.axis_index("ctx"), lax.axis_index("head")
    source = source if piece_rows % 16 == 0 else source[...].astype(f32)
    rows = unfold(source[:start, :], cat_width, on).astype(keys_ref.dtype)
    for s in range(2):
        row = pl.multiple_of(span_ref[s, me ^ side] * span, span)
        keys_ref[pl.ds(row, span), :] = rows[s * span : (s + 1) * span, :]
    for m in range(head_count):
        quarter = head ^ m
        for k in range(1, z_count):
            owner = 2 * (me // 2 ^ k) + lax.rem(me + side, 2)
            row = span_ref[quarter // per_span, owner] * span + lax.rem(quarter, per_span) * piece_rows
            rows = unfold(source[start : start + size, :], cat_width, on)
            keys_ref[pl.ds(pl.multiple_of(row, piece_rows), piece_rows), :] = rows.astype(keys_ref.dtype)
            start += size


def attend_kernel(head_count, *refs):
    span_ref, sib_pieces, placed_ref, q_ref, dl_ref = refs[:5]
    keys_ref, ds_ref, send_ref, score_part, prob_part, e_scr, prob_scr = refs[5:]
    half_count, row_count, cat_width = q_ref.shape
    lat_width = dl_ref.shape[2]
    total = keys_ref.shape[0]
    tile_count = total // key_tile
    span = total // lax.axis_size("ctx") // 2
    me = lax.axis_index("ctx")
    if placed_ref.dtype == keys_ref.dtype:
        place_rows(head_count, 1, span_ref, sib_pieces, keys_ref)
    else:
        place_rows(head_count, 1, span_ref, sib_pieces, placed_ref)
        keys_ref[...] = placed_ref[...].astype(bf16)

    my_lower, my_upper = span_ref[0, me], span_ref[1, me]
    chunks = [slice(n, n + min(row_chunk, row_count)) for n in range(0, row_count, row_chunk)]
    groups = tile_groups(tile_count)
    counts = [last - first for first, last in groups]
    tiles = [slice(first * key_tile, last * key_tile) for first, last in groups]
    places = [tile_place(first, tile_count, span, my_lower) for first, last in groups]
    work = [(g, chunk) for g in range(len(groups)) for chunk in chunks]
    step_shape = (key_tile, min(row_chunk, row_count))
    key_step = lax.broadcasted_iota(jnp.int32, step_shape, 0)
    row_step = lax.rem(lax.broadcasted_iota(jnp.int32, step_shape, 1), span)
    step = row_step - key_step

    def score_dot(u, chunk):
        is_upper, kt = places[u]
        return dot_nt(keys_ref[tile_rows(kt, counts[u]), :], q_ref[half_of(is_upper), chunk])

    top_parts, sum_parts = {}, {}
    ahead = [score_dot(*item) for item in work[:dots_ahead]]
    for i, (u, chunk) in enumerate(work):
        scores = ahead.pop(0)
        if i + dots_ahead < len(work):
            ahead.append(score_dot(*work[i + dots_ahead]))
        is_upper, kt = places[u]
        if groups[u][0] >= tile_count // 2:
            base = kt * key_tile - pick(is_upper, my_upper, my_lower) * span
            scores = jnp.where(step >= base, scores, neg_big)
        top = jnp.max(scores, axis=0, keepdims=True)
        weights = jnp.exp2(scores - top)
        e_scr[tiles[u], chunk] = weights
        top_parts.setdefault(u, []).append(top)
        sum_parts.setdefault(u, []).append(jnp.sum(weights, axis=0, keepdims=True))
    tops = [jnp.concatenate(top_parts[u], axis=1) for u in range(len(groups))]
    sums = [jnp.concatenate(sum_parts[u], axis=1) for u in range(len(groups))]

    def prob_dot(u, chunk):
        is_upper, kt = places[u]
        return dot_nt(keys_ref[tile_rows(kt, counts[u]), :lat_width], dl_ref[half_of(is_upper), chunk])

    ahead = [prob_dot(*item) for item in work[:dots_ahead]]
    row_top, row_sum = [], []
    for s in range(2):
        kept = [jnp.where(half_of(is_upper) == s, top, neg_big) for (is_upper, kt), top in zip(places, tops)]
        best = functools.reduce(jnp.maximum, kept)
        row_top.append(best)
        row_sum.append(functools.reduce(jnp.add, [jnp.exp2(top - best) * add for top, add in zip(kept, sums)]))
    inverse = [1.0 / part for part in row_sum]
    factors = []
    for (is_upper, kt), top in zip(places, tops):
        best = pick(is_upper, row_top[1], row_top[0])
        factors.append(jnp.exp2(top - best) * pick(is_upper, inverse[1], inverse[0]))
    deltas = []
    for s in range(2):
        parts = dl_ref[s, row_count:, :].astype(f32)
        width = min(lat_width, row_count)
        rows = [parts[j : j + 1, :width] + parts[8 + j : 9 + j, :width] for j in range(row_count // width)]
        deltas.append(jnp.concatenate(rows, axis=1))
    sure = (tile_count // 2 + 1) * key_tile
    score_part[sure:, :] = jnp.zeros((total - sure, cat_width), f32)
    prob_part[sure:, :] = jnp.zeros((total - sure, lat_width), f32)

    def key_grads(u, source, target, rhs, first, last):
        is_upper, kt = places[u]
        part = dot_nn(source[...], rhs[half_of(is_upper), :row_count, first:last])
        if groups[u][0] <= tile_count // 2:
            target[tile_rows(kt, counts[u]), first:last] = part
        else:
            target[tile_rows(kt, counts[u]), first:last] += part

    def key_steps(u):
        widths = [(first, min(first + 256, cat_width)) for first in range(0, cat_width, 256)]
        steps = []
        for first, last in widths:
            steps.append(functools.partial(key_grads, u, ds_ref.at[tiles[u]], score_part, q_ref, first, last))
            if last <= lat_width:
                steps.append(functools.partial(key_grads, u, prob_scr.at[u % 2, : counts[u] * key_tile], prob_part, dl_ref, first, last))
        return steps

    pending = []
    for i, (u, chunk) in enumerate(work):
        d_prob = ahead.pop(0)
        if i + dots_ahead < len(work):
            ahead.append(prob_dot(*work[i + dots_ahead]))
        left = len(chunks) - i % len(chunks)
        for j in range(-(-len(pending) // left)):
            pending.pop(0)()
        is_upper, kt = places[u]
        delta = pick(is_upper, deltas[1], deltas[0])
        prob = e_scr[tiles[u], chunk] * factors[u][:, chunk]
        ds_ref[tiles[u], chunk] = (prob * (d_prob - delta[:, chunk])).astype(bf16)
        prob_scr[u % 2, : counts[u] * key_tile, chunk] = prob.astype(bf16)
        if left == 1:
            pending = key_steps(u)
    for key_step in pending:
        key_step()

    pack(1, head_count, span_ref, score_part, prob_part, send_ref)


def pack(side, head_count, span_ref, score_part, prob_part, out_ref):
    total, cat_width = score_part.shape
    lat_width = prob_part.shape[1]
    z_count = lax.axis_size("ctx") // 2
    piece_rows = total // z_count // 2 // head_count
    span = total // z_count // 4
    per_span = span // piece_rows
    on = piece_rows % 32 == 0
    size = z_count * folded(piece_rows, cat_width, on)[0]
    owner_core = lax.rem(lax.axis_index("ctx") + side, 2)
    for quarter in range(head_count):
        rows = []
        for other in range(z_count):
            block = span_ref[quarter // per_span, 2 * other + owner_core]
            start = block * span + quarter % per_span * piece_rows
            here = pl.ds(pl.multiple_of(start, piece_rows), piece_rows)
            terms = score_part[here, :] * (1.0 / log2_e)
            latent = terms[:, :lat_width] + prob_part[here, :]
            rows.append(fold(jnp.concatenate([latent, terms[:, lat_width:]], axis=1), on))
        out_ref[quarter * size : (quarter + 1) * size, :] = jnp.concatenate(rows, axis=0).astype(bf16)


def query_kernel(
    scale, span_ref, keys_ref, ds_ref, w_uk_ref, nope_ref, rope_ref, dq_scr
):
    tile_total, row_count = ds_ref.shape[0] // key_tile, ds_ref.shape[1]
    tile_count = tile_total - 1
    heads, nope_width, lat_width = w_uk_ref.shape
    span = row_count // heads
    cat_width = keys_ref.shape[1]
    my_lower = span_ref[0, lax.axis_index("ctx")]
    places = [tile_place(u, tile_count, span, my_lower) for u in range(tile_total)]
    sure = tile_count // 2 + 1
    dq_scr[1] = dot_tn(keys_ref[: sure * key_tile, :], ds_ref[: sure * key_tile, :])
    dq_scr[0] = dot_tn(keys_ref[:key_tile, :], ds_ref[tile_count * key_tile :, :])
    for u, (is_upper, kt) in enumerate(places):
        if not isinstance(is_upper, bool):
            dq_scr[half_of(is_upper)] += dot_tn(keys_ref[tile_rows(kt), :], ds_ref[tile_rows(u), :])
    for pair in range(heads // 2):
        wide = slice(pair * 2 * span, (pair + 1) * 2 * span)
        turned = [jnp.transpose(dq_scr[s, :, wide]) * scale for s in range(2)]
        for p in range(2):
            head = 2 * pair + p
            rows = jnp.concatenate([t[p * span : (p + 1) * span, :lat_width] for t in turned], axis=0)
            nope_ref[:, head * nope_width : (head + 1) * nope_width] = dot_nt(
                rows.astype(bf16), w_uk_ref[head]
            ).astype(bf16)
        rope = [
            jnp.concatenate([t[p * span : (p + 1) * span, lat_width:] for t in turned], axis=0) for p in range(2)
        ]
        width = 2 * (cat_width - lat_width)
        rope_ref[:, pair * width : (pair + 1) * width] = jnp.concatenate(rope, axis=1).astype(bf16)


def pair_sum_kernel(keep_ref, recv_ref, own_ref, *send_refs):
    head = lax.axis_index("head")
    share = own_ref.shape[0]

    def both(target):
        rows = pl.ds(pl.multiple_of(target * share, share), share)
        return keep_ref[rows, :].astype(f32) + recv_ref[rows, :].astype(f32)

    own_ref[...] = both(head)
    for m, ref in zip(range(len(send_refs), 0, -1), send_refs):
        ref[...] = both(head ^ m).astype(bf16)


def head_sum_kernel(*refs):
    z_count = refs[0].shape[0] // refs[-2].shape[0]
    head_count = len(refs) - 1 - z_count
    terms, own_ref, send_refs, total = refs[:head_count], refs[head_count], refs[head_count + 1 : -1], refs[-1]
    total[...] = functools.reduce(jnp.add, [ref[...].astype(f32) for ref in terms])
    rows = own_ref.shape[0]
    z = lax.axis_index("ctx") // 2

    def share(k):
        return total[pl.ds(pl.multiple_of((z ^ k) * rows, rows), rows), :]

    own_ref[...] = share(0)
    for k, ref in zip(range(len(send_refs), 0, -1), send_refs):
        ref[...] = share(k).astype(bf16)


def chip_sum_kernel(*refs):
    refs[-1][...] = functools.reduce(jnp.add, [ref[...].astype(f32) for ref in refs[:-1]]).astype(bf16)


def norm_back_kernel(cache_t_ref, gain_ref, *refs):
    shares, (out_hbm, total, out_ref, sems) = refs[:-4], refs[-4:]
    head = lax.axis_index("head")
    rows = total.shape[0] // len(shares)
    lat_width = gain_ref.shape[0]
    for m, ref in enumerate(shares):
        total[pl.ds(pl.multiple_of((head ^ m) * rows, rows), rows), :] = unfold(
            ref[...].astype(f32), total.shape[1], rows % 32 == 0
        )
    blocks = [slice(j, min(j + 128, total.shape[1])) for j in range(0, total.shape[1], 128)]
    copies = [pltpu.make_async_copy(out_ref.at[b], out_hbm.at[b], sems.at[j]) for j, b in enumerate(blocks)]
    values = cache_t_ref[:lat_width, :].astype(f32)
    inverse = lax.rsqrt(jnp.mean(values * values, axis=0, keepdims=True) + eps_norm)
    out_ref[lat_width:, :] = jnp.transpose(total[:, lat_width:])
    copies[-1].start()
    scaled = jnp.transpose(total[:, :lat_width] * gain_ref[...].astype(f32)[None, :])
    inner = jnp.mean(values * scaled, axis=0, keepdims=True)
    factor = inverse * inverse * inverse * inner
    for block, copy in zip(blocks[:-1], copies):
        out_ref[block, :] = inverse * scaled[block] - values[block] * factor
        copy.start()
    for copy in copies:
        copy.wait()


def local(q_nope, q_rope, kv_cache, kv_gain, w_uk, w_uv, attn_out, d_out, span_table):
    shape = jax.ShapeDtypeStruct
    tok_rows, cat_width = kv_cache.shape
    heads, nope_width, lat_width = w_uk.shape
    value_width = w_uv.shape[2]
    rope_width = q_rope.shape[1] // heads
    span = tok_rows // 2
    row_count = span * heads
    scale = float(nope_width + rope_width) ** (-0.5)
    ctx_count, head_count = lax.axis_size("ctx"), lax.axis_size("head")
    z_count = ctx_count // 2
    total = ctx_count * tok_rows
    tile_total = total // key_tile + 1
    piece_rows = tok_rows // head_count
    cache_t = kv_cache.T
    spans = span_table.T

    def to_core(rows):
        return lax.ppermute(rows, "ctx", [(i, i ^ 1) for i in range(ctx_count)])

    def to_chip(rows, k):
        return lax.ppermute(rows, "ctx", [(i, i ^ (2 * k)) for i in range(ctx_count)])

    def to_head(rows, m):
        return lax.ppermute(rows, "head", [(j, j ^ m) for j in range(head_count)])

    on = piece_rows % 32 == 0
    piece = pl.pallas_call(
        piece_kernel,
        out_shape=shape(folded(piece_rows, cat_width, on), bf16),
        in_specs=[in_any],
        out_specs=in_vmem,
        scratch_shapes=[
            pltpu.VMEM((cat_width, tok_rows), bf16),
            pltpu.VMEM((tok_rows, cat_width), f32),
            pltpu.SemaphoreType.DMA,
        ],
        compiler_params=params(piece_mib),
        name="piece",
    )(cache_t)
    pieces = [to_chip(piece, k) for k in range(1, z_count)]
    keys_own = pl.pallas_call(
        functools.partial(own_kernel, on),
        out_shape=shape(folded(tok_rows, cat_width, on), bf16),
        in_specs=[in_vmem] * 2,
        out_specs=in_vmem,
        compiler_params=params(8),
        cost_estimate=pl.CostEstimate(flops=window_flops, bytes_accessed=mib, transcendentals=0),
        name="own_keys",
    )(cache_t, kv_gain)
    *pieces, keys_own = lax.optimization_barrier((*pieces, keys_own))
    pieces = pl.pallas_call(
        functools.partial(join_chips_kernel, on, cat_width),
        out_shape=shape(((z_count - 1) * piece.shape[0], piece.shape[1]), bf16),
        in_specs=[in_vmem] * z_count,
        out_specs=in_vmem,
        compiler_params=params(8),
        name="join_chips",
    )(kv_gain, *pieces)

    def join(rows, name):
        return pl.pallas_call(
            join_kernel,
            out_shape=shape((sum(r.shape[0] for r in rows), rows[0].shape[1]), bf16),
            in_specs=[in_vmem] * len(rows),
            out_specs=in_vmem,
            compiler_params=params(4),
            name=name,
        )(*rows)

    queries, d_latent = pl.pallas_call(
        functools.partial(project_kernel, scale * log2_e),
        out_shape=(shape((2, row_count, cat_width), bf16), shape((2, row_count + delta_rows, lat_width), bf16)),
        in_specs=[in_vmem] * 6 + [in_any],
        out_specs=(in_vmem,) * 2,
        scratch_shapes=[pltpu.VMEM((heads // 2, 2, 8, 2 * span), f32)],
        compiler_params=params(project_mib),
        cost_estimate=pl.CostEstimate(
            flops=8 * row_count * nope_width * lat_width, bytes_accessed=12 * mib, transcendentals=0
        ),
        name="project",
    )(q_nope, q_rope, w_uk, d_out, attn_out, w_uv, pieces)
    pieces = [pieces] + [to_head(pieces, m) for m in range(1, head_count)]
    *pieces, queries, d_latent = lax.optimization_barrier((*pieces, queries, d_latent))
    pieces = join([keys_own] + pieces, "join_heads")
    sib_pieces = to_core(pieces)
    aligned = piece_rows % 16 == 0
    placed = pl.pallas_call(
        functools.partial(place_rows, head_count, 0),
        out_shape=shape((total, cat_width), bf16 if aligned else f32),
        in_specs=[in_smem, in_vmem],
        out_specs=in_vmem,
        compiler_params=params(8),
        name="place",
    )(spans, pieces)
    sib_pieces, placed = lax.optimization_barrier((sib_pieces, placed))

    piece_shape = piece.shape
    share_shape = (z_count * piece_shape[0], piece_shape[1])
    all_shape = (head_count * share_shape[0], piece_shape[1])
    keys, d_score, send, score_part, prob_part = pl.pallas_call(
        functools.partial(attend_kernel, head_count),
        out_shape=(
            shape((total, cat_width), bf16),
            shape((tile_total * key_tile, row_count), bf16),
            shape(all_shape, bf16),
            shape((total, cat_width), f32),
            shape((total, lat_width), f32),
        ),
        in_specs=[in_smem] + [in_vmem] * 4,
        input_output_aliases={2: 0} if aligned else {},
        out_specs=(in_vmem,) * 5,
        scratch_shapes=[
            pltpu.VMEM((tile_total * key_tile, row_count), f32),
            pltpu.VMEM((2, key_tile, row_count), bf16),
        ],
        compiler_params=params(attend_mib if total <= 2048 else 56),
        cost_estimate=pl.CostEstimate(
            flops=2 * tile_total * key_tile * row_count * (2 * cat_width + 2 * lat_width),
            bytes_accessed=12 * mib,
            transcendentals=tile_total * key_tile * row_count,
        ),
        name="attend",
    )(spans, sib_pieces, placed, queries, d_latent)

    recv = to_core(send)
    keep = pl.pallas_call(
        functools.partial(pack, 0, head_count),
        out_shape=shape(all_shape, bf16),
        in_specs=[in_smem] + [in_vmem] * 2,
        out_specs=in_vmem,
        compiler_params=params(6),
        name="pack_keep",
    )(spans, score_part, prob_part)
    sums = pl.pallas_call(
        pair_sum_kernel,
        out_shape=(shape(share_shape, f32),) + (shape(share_shape, bf16),) * (head_count - 1),
        in_specs=[in_vmem] * 2,
        out_specs=(in_vmem,) * head_count,
        compiler_params=params(4),
        name="pair_sum",
    )(keep, recv)
    *sums, d_score = lax.optimization_barrier((*sums, d_score))
    d_q_nope, d_q_rope = pl.pallas_call(
        functools.partial(query_kernel, scale),
        out_shape=(shape(q_nope.shape, bf16), shape(q_rope.shape, bf16)),
        in_specs=[in_smem] + [in_vmem] * 3,
        out_specs=(in_vmem,) * 2,
        scratch_shapes=[pltpu.VMEM((2, cat_width, row_count), f32)],
        compiler_params=params(query_mib),
        cost_estimate=pl.CostEstimate(
            flops=2 * tile_total * key_tile * row_count * cat_width,
            bytes_accessed=8 * mib,
            transcendentals=0,
        ),
        name="query_grads",
    )(spans, keys, d_score, w_uk)
    terms = [sums[0]] + [to_head(rows, m) for m, rows in zip(range(head_count - 1, 0, -1), sums[1:])]
    *terms, d_q_nope, d_q_rope = lax.optimization_barrier((*terms, d_q_nope, d_q_rope))
    sums = pl.pallas_call(
        head_sum_kernel,
        out_shape=(shape(piece_shape, f32),) + (shape(piece_shape, bf16),) * (z_count - 1),
        in_specs=[in_vmem] * head_count,
        out_specs=(in_vmem,) * z_count,
        scratch_shapes=[pltpu.VMEM(share_shape, f32)],
        compiler_params=params(4),
        name="head_sum",
    )(*terms)
    terms = [sums[0]] + [to_chip(rows, k) for k, rows in zip(range(z_count - 1, 0, -1), sums[1:])]
    share = pl.pallas_call(
        chip_sum_kernel,
        out_shape=shape(piece_shape, bf16),
        in_specs=[in_vmem] * z_count,
        out_specs=in_vmem,
        compiler_params=params(4),
        name="chip_sum",
    )(*terms)
    shares = [share] + [to_head(share, m) for m in range(1, head_count)]
    d_cache_t = pl.pallas_call(
        norm_back_kernel,
        out_shape=shape((cat_width, tok_rows), f32),
        in_specs=[in_vmem] * (2 + head_count),
        out_specs=in_any,
        scratch_shapes=[
            pltpu.VMEM((tok_rows, cat_width), f32),
            pltpu.VMEM((cat_width, tok_rows), f32),
            pltpu.SemaphoreType.DMA((-(-cat_width // 128),)),
        ],
        compiler_params=params(8),
        name="norm_back",
    )(cache_t, kv_gain, *shares)
    return (d_q_nope, d_q_rope, d_cache_t.T)


def solution(mesh):
    in_specs = (
        P("ctx", "head"),
        P("ctx", "head"),
        P("ctx", None),
        P(),
        P("head", None, None),
        P("head", None, None),
        P("ctx", "head"),
        P("ctx", "head"),
        P(),
    )
    out_specs = (P("ctx", "head"), P("ctx", "head"), P("ctx", None))
    return jax.shard_map(local, mesh=mesh, in_specs=in_specs, out_specs=out_specs, check_vma=False)
```
